32 devices in a mesh: grp: 2 (over y), row: 8 (over z, x), col: 2 (over core).
Axes of the slice: x: 2, y: 2, z: 4, core: 2. Of those that a mesh axis runs over, the one named last changes fastest.
Arguments:
- feats: bfloat16 [128, 128, 256], P(('grp', 'row'), 'col'), parts along dimension 0, may hold values from -6 to 6
- weight: bfloat16 [256, 256], replicated, may hold values from -0.375 to 0.375
- degree: int32 [128, 128], P(('grp', 'row'), 'col'), parts along dimension 0, may hold values from 0 to 63
- tile_cols: int32 [128, 16], P(('grp', 'row')), parts along dimension 0, may hold values from -1 to 63, as said below
- adjacency: int32 [2048, 128, 128], P(('grp', 'row'), 'col'), parts along dimension 0, may hold values 0 or 1
- cotangent: bfloat16 [128, 128, 256], P(('grp', 'row'), 'col'), parts along dimension 0, may hold values from -6 to 6
Outputs:
- output: bfloat16 [128, 128, 256], P(('grp', 'row'), 'col'), parts along dimension 0
- grad_feats: bfloat16 [128, 128, 256], P(('grp', 'row'), 'col'), parts along dimension 0
The draws below stay inside these ranges and needn't reach their ends.
There are 2 independent parts, one for each index of `grp`. The reference program is written for one: setup_inputs(seed, part) draws one part's arguments, and reference() takes and returns one part's arrays. A program takes and returns all parts, laid end to end along the dimension named above; an argument that names none is the same for every part. Nothing has to cross between parts.
Inputs may be any that keep to these rules, and one draw needn't show every extreme that they name: `tile_cols`: in each row block's list the live slots (not -1) come first, at least one of them. Among the live slots of the 8 row blocks of one index of row, at most 16 have column blocks c with the same c // 8.
All inputs are finite; a program needn't handle non-finite values. No bound on the sum of `adjacency` on one device may be relied on, other than what follows from the above.
Results may differ from the reference program's by a relative error of at most 0.0063.
Values may be sent and summed in bfloat16 or wider, within the bound.
No kernel may reach another device: no remote copies, remote signals or barrier semaphores. Data moves between devices by JAX's collectives and lax.ppermute only.
A program may use at most 64 MiB of HBM per device.

```python
import jax
import jax.numpy as jnp
from jax import lax

F = 256
BS = 128
K = 16
BLK_DEV = 8
NB = 64
MOST = 16
N_ROW = 8


def draw_tile_cols(key, part):
    key = jax.random.fold_in(key, 7)
    low_count = max(1, (MOST + BLK_DEV - 1) // BLK_DEV)
    light_top = max(low_count, K // 4)
    heavy_low = max(low_count, K // 2)
    subkeys = jax.random.split(key, 6)
    target_row = jax.random.randint(subkeys[0], (), 0, N_ROW)
    forced_row = jax.random.randint(subkeys[1], (), 0, N_ROW)
    row_ids = jnp.arange(N_ROW)
    is_heavy = (jax.random.randint(subkeys[2], (N_ROW,), 0, 8) == 0) | (row_ids == forced_row)
    light_len = jax.random.randint(subkeys[3], (N_ROW, BLK_DEV), low_count, light_top + 1)
    heavy_len = jax.random.randint(subkeys[4], (N_ROW, BLK_DEV), heavy_low, K + 1)
    first_block = (row_ids[:, None] == forced_row) & (jnp.arange(BLK_DEV)[None, :] == 0)
    heavy_len = jnp.where(first_block, K, heavy_len)
    lengths = jnp.where(is_heavy[:, None], heavy_len, light_len)

    def one_device(dev_key, dev_len):
        key_owner, key_local = jax.random.split(dev_key)
        is_live = (jnp.arange(K)[None, :] < dev_len[:, None]).reshape(-1)
        live_order = jnp.argsort(1 - is_live.astype(jnp.int32), stable=True)
        position = jnp.zeros((BLK_DEV * K,), jnp.int32).at[live_order].set(jnp.arange(BLK_DEV * K, dtype=jnp.int32))
        shuffle = jax.random.permutation(key_owner, N_ROW)
        owners = (shuffle[position // MOST] - shuffle[0] + target_row) % N_ROW
        local_index = jax.random.randint(key_local, (BLK_DEV * K,), 0, BLK_DEV)
        drawn = jnp.where(is_live, owners * BLK_DEV + local_index, -1)
        return drawn.reshape(BLK_DEV, K)
    result = jax.vmap(one_device)(jax.random.split(subkeys[5], N_ROW), lengths)
    return result.reshape(N_ROW * BLK_DEV, K).astype(jnp.int32)


def plant(entries, key, least, largest):
    place = [jax.random.randint(jax.random.fold_in(key, axis), (), 0, length) for axis, length in enumerate(entries.shape)]
    longest = entries.shape.index(max(entries.shape))
    next_to = place[:longest] + [(place[longest] + 1) % entries.shape[longest]] + place[longest + 1:]
    return entries.at[tuple(place)].set(least).at[tuple(next_to)].set(largest)


def level_of(rng, dims, cuts, least, largest):
    factor_of, own = 1.0, jax.random.fold_in(rng, 6)
    for axis_at, parts in cuts:
        steps = jnp.exp(jax.random.uniform(jax.random.fold_in(own, axis_at), (parts,), jnp.float32, least / len(cuts), largest / len(cuts)))
        factor_of = factor_of * jnp.repeat(steps, dims[axis_at] // parts).reshape([-1 if axis == axis_at else 1 for axis in range(len(dims))])
    return factor_of


def noise(own_key, shape, spread, reach, cuts=(), kind=jnp.bfloat16):
    values = jax.random.normal(own_key, shape, jnp.float32) * spread
    if len(cuts) > 0:
        values = level_of(own_key, shape, cuts, -0.22, 0.18) * values
    return jnp.clip(values, min=-reach, max=reach).astype(kind)


def setup_inputs(seed: int = 0, part: int = 0) -> dict:
    key_of = jax.random.split(jax.random.key(seed), 7)
    part_keys = jax.random.split(jax.random.fold_in(key_of[6], part), 7)
    feats = noise(part_keys[0], (NB, BS, F), 1.0, 6.0, ((0, 8), (1, 2)))
    weight = noise(key_of[1], (F, F), F ** -0.5, 0.375)
    degree = plant(jax.random.randint(part_keys[2], (NB, BS), 0, 64), jax.random.fold_in(part_keys[2], 1), 0, 63).astype(jnp.int32)
    tile_cols = draw_tile_cols(jax.random.fold_in(jax.random.fold_in(key_of[6], part), 71), part)
    adjacency = plant((jax.random.randint(part_keys[4], (NB * K, BS, BS), 0, 4) < 1).astype(jnp.int32), jax.random.fold_in(part_keys[4], 1), 0, 1)
    cotangent = noise(part_keys[5], (NB, BS, F), 1.0, 6.0, ((0, 8), (1, 2)))
    return dict(feats=feats, weight=weight, degree=degree, tile_cols=tile_cols, adjacency=adjacency, cotangent=cotangent)


def reference(feats, weight, degree, tile_cols, adjacency, cotangent):
    scaling = lax.rsqrt(degree.astype(jnp.float32) + 1.0)[..., None]
    projected = jnp.dot(feats.reshape(NB * BS, F), weight, preferred_element_type=jnp.float32).reshape(NB, BS, F)
    sent_rows = (scaling * projected).astype(jnp.bfloat16)
    row_cols = tile_cols.reshape(N_ROW, BLK_DEV, K)
    tile_adj = adjacency.reshape(N_ROW, BLK_DEV, K, BS, BS)

    def forward(current, tile_item):
        cols_dev, adj_dev = tile_item
        is_live = cols_dev >= 0
        picked = jnp.take(sent_rows, jnp.where(is_live, cols_dev, 0), axis=0).astype(jnp.float32)
        picked = picked * is_live[..., None, None].astype(jnp.float32)
        return (current, jnp.einsum('bkji,bkjf->bif', adj_dev.astype(jnp.float32), picked))
    _, gathered = lax.scan(forward, jnp.zeros((), jnp.float32), (row_cols, tile_adj))
    gathered = gathered.reshape(NB, BS, F)
    mixed = scaling * (gathered + sent_rows.astype(jnp.float32))
    sigmoid_z = jax.nn.sigmoid(mixed)
    output = (mixed * sigmoid_z).astype(jnp.bfloat16)
    silu_slope = sigmoid_z * (1.0 + mixed * (1.0 - sigmoid_z))
    back_sent = (scaling * cotangent.astype(jnp.float32) * silu_slope).astype(jnp.bfloat16)
    grad_rows_dev = back_sent.reshape(N_ROW, BLK_DEV, BS, F)

    def backward(back_total, tile_item):
        cols_dev, adj_dev, rows_dev = tile_item
        partials = jnp.einsum('bkji,bif->bkjf', adj_dev.astype(jnp.float32), rows_dev.astype(jnp.float32))
        drop_index = jnp.where(cols_dev >= 0, cols_dev, NB).reshape(-1).astype(jnp.int32)
        return (back_total.at[drop_index].add(partials.reshape(BLK_DEV * K, BS, F)), None)
    back_total, _ = lax.scan(backward, jnp.zeros((NB + 1, BS, F), jnp.float32), (row_cols, tile_adj, grad_rows_dev))
    returned = back_total[:NB]
    combined = (scaling * (returned + back_sent.astype(jnp.float32))).astype(jnp.bfloat16)
    grad_feats = jnp.dot(combined.reshape(NB * BS, F), weight.T, preferred_element_type=jnp.float32)
    return (output, grad_feats.astype(jnp.bfloat16).reshape(NB, BS, F))
```

```python
import functools

import jax
import jax.numpy as jnp
from jax import lax
from jax.experimental import pallas as pl
from jax.experimental.pallas import tpu as pltpu
from jax.sharding import PartitionSpec as P

F32 = jnp.float32
BF16 = jnp.bfloat16


def sparse_plan(feats, weight, degree, tile_cols, adjacency, cotangent):
    blocks, half_rows, feat_width = feats.shape
    slots_per = tile_cols.shape[1]
    tile_side = adjacency.shape[2]
    peer_count = lax.axis_size("row")
    tile_count = blocks * slots_per
    per_peer = (tile_count + peer_count - 1) // peer_count
    capacity = peer_count * per_peer
    columns = tile_cols.reshape(tile_count)
    is_live = columns >= 0
    owners = jnp.where(is_live, columns // blocks, -1)
    local_block = jnp.where(is_live, columns % blocks, -1)
    earlier = jnp.arange(tile_count)[:, None] > jnp.arange(tile_count)[None, :]
    same_owner = (owners[:, None] == owners[None, :]) & earlier & is_live[None, :]
    tile_rank = jnp.sum(same_owner.astype(jnp.int32), axis=1)
    target_slot = jnp.where(is_live, owners * per_peer + tile_rank, capacity)
    wanted = jnp.zeros((capacity,), jnp.int32).at[target_slot].set(local_block + 1, mode="drop")
    wanted = wanted.reshape(peer_count, per_peer)
    received = lax.all_to_all(wanted, "row", split_axis=0, concat_axis=0, tiled=True)
    incoming = received - 1
    scaling = lax.rsqrt(degree.astype(F32) + 1.0)[..., None]
    projected = jnp.dot(
        feats.reshape(blocks * half_rows, feat_width), weight, preferred_element_type=F32
    )
    sent_rows = (scaling * projected.reshape(blocks, half_rows, feat_width)).astype(BF16)
    tiles_bf = adjacency.astype(BF16).reshape(blocks, slots_per, half_rows, tile_side)
    pick_index = jnp.where(incoming < 0, blocks, incoming)
    replies = jnp.take(sent_rows, pick_index, axis=0, mode="fill", fill_value=0)
    fetched = lax.all_to_all(replies, "row", split_axis=0, concat_axis=0, tiled=True).reshape(
        capacity, half_rows, feat_width
    )
    tile_feats = jnp.take(fetched, target_slot, axis=0, mode="fill", fill_value=0)
    tile_feats = tile_feats.reshape(blocks, slots_per, half_rows, feat_width)
    gathered = lax.dot_general(
        tiles_bf, tile_feats, (((1, 2), (1, 2)), ((0,), (0,))), preferred_element_type=F32
    )
    own_rows = lax.psum_scatter(gathered, "col", scatter_dimension=1, tiled=True)
    mixed = scaling * (own_rows + sent_rows.astype(F32))
    sigmoid_z = jax.nn.sigmoid(mixed)
    output = (mixed * sigmoid_z).astype(BF16)
    silu_slope = sigmoid_z * (1.0 + mixed * (1.0 - sigmoid_z))
    back_sent = (scaling * cotangent.astype(F32) * silu_slope).astype(BF16)
    full_rows = lax.all_gather(back_sent, "col", axis=1, tiled=True)
    partials = lax.dot_general(
        tiles_bf, full_rows, (((3,), (1,)), ((0,), (0,))), preferred_element_type=F32
    )
    outgoing = jnp.zeros((capacity, half_rows, feat_width), F32)
    outgoing = outgoing.at[target_slot].set(
        partials.reshape(tile_count, half_rows, feat_width), mode="drop"
    )
    outgoing = outgoing.reshape(peer_count, per_peer, half_rows, feat_width)
    arrived = lax.all_to_all(outgoing, "row", split_axis=0, concat_axis=0, tiled=True).reshape(
        capacity, half_rows, feat_width
    )
    selector = (incoming.reshape(capacity)[:, None] == jnp.arange(blocks)[None, :]).astype(F32)
    returned = jnp.einsum("sl,sjf->ljf", selector, arrived, precision=lax.Precision.HIGHEST)
    combined = (scaling * (returned + back_sent.astype(F32))).astype(BF16)
    grad_rows = jnp.dot(
        combined.reshape(blocks * half_rows, feat_width), weight.T, preferred_element_type=F32
    )
    return (output, grad_rows.astype(BF16).reshape(blocks, half_rows, feat_width))


VM = pl.BlockSpec(memory_space=pltpu.VMEM)
SM = pl.BlockSpec(memory_space=pltpu.SMEM)


def call(body, outs, ins, args, flops, nbytes, name, **kw):
    return pl.pallas_call(
        body,
        out_shape=outs,
        in_specs=ins,
        out_specs=jax.tree.map(lambda _: VM, outs),
        cost_estimate=pl.CostEstimate(flops=flops, bytes_accessed=nbytes, transcendentals=0),
        compiler_params=pltpu.CompilerParams(vmem_limit_bytes=24 * 2**20),
        name=name,
        **kw,
    )(*args)


def dense_plan(feats, weight, degree, tile_cols, adjacency, cotangent):
    blocks, half, width = feats.shape
    slots = tile_cols.shape[1]
    side = adjacency.shape[2]
    n = lax.axis_size("row")
    rows = blocks * half
    hrows = rows // 2
    span = blocks * side
    far = n // 2
    ring = [2 * p if p < far else 2 * (n - 1 - p) + 1 for p in range(n)]
    fwd = [(ring[p], ring[(p + 1) % n]) for p in range(n)]
    bwd = [(b, a) for a, b in fwd]
    me = lax.axis_index("row")
    z = me // 2
    pos = jnp.where(me % 2 == 0, z, n - 1 - z)
    where_ref = jnp.stack([pos, lax.axis_index("col")]).astype(jnp.int32)

    def owner(where, d):
        p = lax.rem(where[0] + (d + n), n)
        return jnp.where(p < far, 2 * p, 2 * (n - 1 - p) + 1)

    def vout(shape, dtype):
        return jax.ShapeDtypeStruct(shape, dtype)

    def project(deg, x, w, s0, s1, sc):
        proj = jnp.dot(x[...], w[...], preferred_element_type=F32)
        scale = lax.rsqrt(deg[...].astype(F32) + 1.0)
        eye = lax.broadcasted_iota(jnp.int32, (half, half), 0) == lax.broadcasted_iota(
            jnp.int32, (half, half), 1
        )
        for b in range(blocks):
            line = jnp.broadcast_to(scale[b : b + 1, :], (half, half))
            col = jnp.sum(jnp.where(eye, line, 0.0), axis=1, keepdims=True)
            sc[b * half : (b + 1) * half, :] = jnp.broadcast_to(col, (half, 128))
            out = (col * proj[b * half : (b + 1) * half, :]).astype(BF16)
            if b < blocks // 2:
                s0[b * half : (b + 1) * half, :] = out
            else:
                s1[b * half - hrows : (b + 1) * half - hrows, :] = out

    s0, s1, scale = call(
        project,
        (vout((hrows, width), BF16), vout((hrows, width), BF16), vout((rows, 128), F32)),
        [VM] * 3,
        (degree, feats.reshape(rows, width), weight),
        2 * rows * width * width,
        2 * rows * width * 2,
        "project",
    )

    def densify(cols, adj, dense):
        b = pl.program_id(0)
        at = pl.multiple_of(b * side, side)
        dense[:, pl.ds(at, side)] = jnp.zeros((n * rows, side), BF16)

        def add(k, _):
            c = cols[b, k]

            @pl.when(c >= 0)
            def _():
                place = (pl.ds(pl.multiple_of(c * half, half), half), pl.ds(at, side))
                dense[place] = dense[place] + adj[k].astype(F32).astype(BF16)

            return 0

        lax.fori_loop(0, slots, add, 0)

    dense = pl.pallas_call(
        densify,
        out_shape=pltpu.VMEM((n * rows, span), BF16),
        grid=(blocks,),
        in_specs=[SM, pl.BlockSpec((slots, half, side), lambda b: (b, 0, 0))],
        out_specs=VM,
        cost_estimate=pl.CostEstimate(
            flops=0, bytes_accessed=adjacency.size * 4 + 2 * n * rows * span, transcendentals=0
        ),
        compiler_params=pltpu.CompilerParams(
            vmem_limit_bytes=24 * 2**20, dimension_semantics=("arbitrary",)
        ),
        name="densify",
    )(tile_cols, adjacency)

    def shift(x, perm):
        return lax.ppermute(x, "row", perm)

    f0, f1, b0, b1 = [s0], [s1], [s0], [s1]
    for step in range(far):
        f0.append(shift(f0[-1], fwd))
        b1.append(shift(b1[-1], bwd))
        if step < far - 1:
            f1.append(shift(f1[-1], fwd))
            b0.append(shift(b0[-1], bwd))

    def accumulate(where, dense, items, total):
        for d, h, ref in items:
            at = pl.multiple_of(owner(where, d) * rows + h * hrows, hrows)
            term = lax.dot_general(
                ref[...], dense[pl.ds(at, hrows), :], (((0,), (0,)), ((), ())),
                preferred_element_type=F32,
            )
            total = term if total is None else total + term
        return total

    early = [(0, 0, s0), (0, 1, s1)]
    for d in range(1, far):
        early += [(-d, 0, f0[d]), (d, 1, b1[d])]
        if d < far - 1:
            early += [(-d, 1, f1[d]), (d, 0, b0[d])]
    late = [(-(far - 1), 1, f1[far - 1]), (far - 1, 0, b0[far - 1])]
    late += [(-far, 0, f0[far]), (far, 1, b1[far])]

    def gather_early(where, dense, *refs):
        total = refs[-1]
        first = True
        for (d, h, _), ref in zip(early, refs[:-1]):
            term = accumulate(where, dense, [(d, h, ref)], None)
            total[...] = term if first else total[...] + term
            first = False

    def flops_of(items):
        return 2 * hrows * span * width * items

    part = call(
        gather_early,
        vout((width, span), F32),
        [SM] + [VM] * (1 + len(early)),
        (where_ref, dense, *[e[2] for e in early]),
        flops_of(len(early)),
        len(early) * hrows * span * 2,
        "gather_early",
    )

    def gather_late(where, dense, part, *refs):
        keep, give, whole = refs[-3:]
        total = accumulate(where, dense, [(d, h, r) for (d, h, _), r in zip(late, refs)], part[...])
        whole[...] = total.T.reshape(blocks, 2, half, width)
        keep[...] = whole[:, where[1]]
        give[...] = whole[:, 1 - where[1]]

    keep, give = call(
        gather_late,
        (vout((blocks, half, width), F32), vout((blocks, half, width), F32)),
        [SM] + [VM] * (2 + len(late)),
        (where_ref, dense, part, *[e[2] for e in late]),
        flops_of(len(late)),
        len(late) * hrows * span * 2,
        "gather_late",
        scratch_shapes=[pltpu.VMEM((blocks, 2, half, width), F32)],
    )
    other = [(0, 1), (1, 0)]
    got = lax.ppermute(give, "col", other)

    def mix(keep, got, s0, s1, sc, cot, out, back):
        for b in range(blocks):
            own = s0 if b < blocks // 2 else s1
            at = (b * half) % hrows
            s = jnp.tile(sc[b * half : (b + 1) * half, :], (1, width // 128))
            sent = own[at : at + half, :].astype(F32)
            mixed = s * (keep[b] + got[b] + sent)
            sig = jax.nn.sigmoid(mixed)
            out[b] = (mixed * sig).astype(BF16)
            slope = sig * (1.0 + mixed * (1.0 - sig))
            back[b] = (s * cot[b].astype(F32) * slope).astype(BF16)

    output, back = call(
        mix,
        (vout((blocks, half, width), BF16), vout((blocks, half, width), BF16)),
        [VM] * 6,
        (keep, got, s0, s1, scale, cotangent),
        rows * width * 20,
        rows * width * 16,
        "mix",
    )
    peer_back = lax.ppermute(back, "col", other)

    def chunk(where, dense, full, d):
        at = pl.multiple_of(owner(where, d) * rows, rows)
        return jnp.dot(dense[pl.ds(at, rows), :], full, preferred_element_type=F32)

    def return_far(where, dense, back, peer, full, c0, c1):
        q = where[1]
        full[:, q] = back[...]
        full[:, 1 - q] = peer[...]
        out = chunk(where, dense, full[...].reshape(span, width), far).astype(BF16)
        c0[...] = out[:hrows]
        c1[...] = out[hrows:]

    full, far0, far1 = call(
        return_far,
        (
            vout((blocks, 2, half, width), BF16),
            vout((hrows, width), BF16),
            vout((hrows, width), BF16),
        ),
        [SM] + [VM] * 3,
        (where_ref, dense, back, peer_back),
        flops_of(2),
        2 * hrows * span * 2,
        "return_far",
    )
    full = full.reshape(span, width)

    def return_next(where, dense, full, up0, up1, down0, down1):
        up = chunk(where, dense, full[...], far - 1)
        up0[...] = up[:hrows]
        up1[...] = up[hrows:].astype(BF16)
        down = chunk(where, dense, full[...], 1 - far)
        down0[...] = down[:hrows].astype(BF16)
        down1[...] = down[hrows:]

    hshape = (hrows, width)
    up0, up1, down0, down1 = call(
        return_next,
        (vout(hshape, F32), vout(hshape, BF16), vout(hshape, BF16), vout(hshape, F32)),
        [SM] + [VM] * 2,
        (where_ref, dense, full),
        flops_of(4),
        4 * hrows * span * 2,
        "return_next",
    )
    near = [d for d in range(2 - far, far - 1)]

    def return_near(where, dense, full, *outs):
        for d, out in zip(near, outs):
            out[...] = chunk(where, dense, full[...], d)

    chunks = call(
        return_near,
        tuple(vout((rows, width), F32) for _ in near),
        [SM] + [VM] * 2,
        (where_ref, dense, full),
        flops_of(2 * len(near)),
        2 * len(near) * hrows * span * 2,
        "return_near",
    )
    chunks = dict(zip(near, chunks))

    g0, r1 = far0, far1
    g1, r0 = up1, down0
    for step in range(far):
        g0 = shift(g0, fwd)
        r1 = shift(r1, bwd)
        if step < far - 1:
            g1 = shift(g1, fwd)
            r0 = shift(r0, bwd)
        d = far - 1 - step
        if d > 0:
            add0 = up0 if step == 0 else chunks[d][:hrows]
            add1 = down1 if step == 0 else chunks[-d][hrows:]
            g0 = (g0.astype(F32) + add0).astype(BF16)
            r1 = (r1.astype(F32) + add1).astype(BF16)
        if 0 < d - 1:
            g1 = (g1.astype(F32) + chunks[d - 1][hrows:]).astype(BF16)
            r0 = (r0.astype(F32) + chunks[1 - d][:hrows]).astype(BF16)

    def finish(own, g0, g1, r0, r1, back, sc, w, out):
        for h, (g, r) in enumerate(((g0, r0), (g1, r1))):
            at = slice(h * hrows, (h + 1) * hrows)
            total = own[at, :] + g[...].astype(F32) + r[...].astype(F32)
            s = jnp.tile(sc[at, :], (1, width // 128))
            comb = (s * (total + back[at, :].astype(F32))).astype(BF16)
            out[at, :] = lax.dot_general(
                comb, w[...], (((1,), (1,)), ((), ())), preferred_element_type=F32
            ).astype(BF16)

    grad = call(
        finish,
        vout((rows, width), BF16),
        [VM] * 8,
        (chunks[0], g0, g1, r0, r1, back.reshape(rows, width), scale, weight),
        2 * rows * width * width,
        rows * width * 8,
        "finish",
    )
    return output, grad.reshape(blocks, half, width)


def shards(feats, weight, degree, tile_cols, adjacency, cotangent):
    n = lax.axis_size("row")
    blocks, half, width = feats.shape
    dense = (
        n * blocks <= blocks * tile_cols.shape[1]
        and n % 2 == 0
        and n >= 6
        and blocks % 2 == 0
        and half % 16 == 0
        and width % 128 == 0
        and adjacency.shape[2] == 2 * half
        and lax.axis_size("col") == 2
    )
    plan = dense_plan if dense else sparse_plan
    return plan(feats, weight, degree, tile_cols, adjacency, cotangent)


def solution(mesh):
    in_specs = (
        P(("grp", "row"), "col", None),
        P(),
        P(("grp", "row"), "col"),
        P(("grp", "row"), None),
        P(("grp", "row"), "col", None),
        P(("grp", "row"), "col", None),
    )
    out_specs = (P(("grp", "row"), "col", None), P(("grp", "row"), "col", None))
    return jax.shard_map(shards, mesh=mesh, in_specs=in_specs, out_specs=out_specs, check_vma=False)
```

```python
import functools

import jax
import jax.numpy as jnp
from jax import lax
from jax.experimental import pallas as pl
from jax.experimental.pallas import tpu as pltpu
from jax.sharding import PartitionSpec as P

F32 = jnp.float32
BF16 = jnp.bfloat16


def sparse_plan(feats, weight, degree, tile_cols, adjacency, cotangent):
    blocks, half_rows, feat_width = feats.shape
    slots_per = tile_cols.shape[1]
    tile_side = adjacency.shape[2]
    peer_count = lax.axis_size("row")
    tile_count = blocks * slots_per
    per_peer = (tile_count + peer_count - 1) // peer_count
    capacity = peer_count * per_peer
    columns = tile_cols.reshape(tile_count)
    is_live = columns >= 0
    owners = jnp.where(is_live, columns // blocks, -1)
    local_block = jnp.where(is_live, columns % blocks, -1)
    earlier = jnp.arange(tile_count)[:, None] > jnp.arange(tile_count)[None, :]
    same_owner = (owners[:, None] == owners[None, :]) & earlier & is_live[None, :]
    tile_rank = jnp.sum(same_owner.astype(jnp.int32), axis=1)
    target_slot = jnp.where(is_live, owners * per_peer + tile_rank, capacity)
    wanted = jnp.zeros((capacity,), jnp.int32).at[target_slot].set(local_block + 1, mode="drop")
    wanted = wanted.reshape(peer_count, per_peer)
    received = lax.all_to_all(wanted, "row", split_axis=0, concat_axis=0, tiled=True)
    incoming = received - 1
    scaling = lax.rsqrt(degree.astype(F32) + 1.0)[..., None]
    projected = jnp.dot(
        feats.reshape(blocks * half_rows, feat_width), weight, preferred_element_type=F32
    )
    sent_rows = (scaling * projected.reshape(blocks, half_rows, feat_width)).astype(BF16)
    tiles_bf = adjacency.astype(BF16).reshape(blocks, slots_per, half_rows, tile_side)
    pick_index = jnp.where(incoming < 0, blocks, incoming)
    replies = jnp.take(sent_rows, pick_index, axis=0, mode="fill", fill_value=0)
    fetched = lax.all_to_all(replies, "row", split_axis=0, concat_axis=0, tiled=True).reshape(
        capacity, half_rows, feat_width
    )
    tile_feats = jnp.take(fetched, target_slot, axis=0, mode="fill", fill_value=0)
    tile_feats = tile_feats.reshape(blocks, slots_per, half_rows, feat_width)
    gathered = lax.dot_general(
        tiles_bf, tile_feats, (((1, 2), (1, 2)), ((0,), (0,))), preferred_element_type=F32
    )
    own_rows = lax.psum_scatter(gathered, "col", scatter_dimension=1, tiled=True)
    mixed = scaling * (own_rows + sent_rows.astype(F32))
    sigmoid_z = jax.nn.sigmoid(mixed)
    output = (mixed * sigmoid_z).astype(BF16)
    silu_slope = sigmoid_z * (1.0 + mixed * (1.0 - sigmoid_z))
    back_sent = (scaling * cotangent.astype(F32) * silu_slope).astype(BF16)
    full_rows = lax.all_gather(back_sent, "col", axis=1, tiled=True)
    partials = lax.dot_general(
        tiles_bf, full_rows, (((3,), (1,)), ((0,), (0,))), preferred_element_type=F32
    )
    outgoing = jnp.zeros((capacity, half_rows, feat_width), F32)
    outgoing = outgoing.at[target_slot].set(
        partials.reshape(tile_count, half_rows, feat_width), mode="drop"
    )
    outgoing = outgoing.reshape(peer_count, per_peer, half_rows, feat_width)
    arrived = lax.all_to_all(outgoing, "row", split_axis=0, concat_axis=0, tiled=True).reshape(
        capacity, half_rows, feat_width
    )
    selector = (incoming.reshape(capacity)[:, None] == jnp.arange(blocks)[None, :]).astype(F32)
    returned = jnp.einsum("sl,sjf->ljf", selector, arrived, precision=lax.Precision.HIGHEST)
    combined = (scaling * (returned + back_sent.astype(F32))).astype(BF16)
    grad_rows = jnp.dot(
        combined.reshape(blocks * half_rows, feat_width), weight.T, preferred_element_type=F32
    )
    return (output, grad_rows.astype(BF16).reshape(blocks, half_rows, feat_width))


VM = pl.BlockSpec(memory_space=pltpu.VMEM)
ANY = pl.BlockSpec(memory_space=pl.ANY)
OTHER = [(0, 1), (1, 0)]


def call(body, outs, ins, args, flops, nbytes, name, **kw):
    return pl.pallas_call(
        body,
        out_shape=outs,
        in_specs=ins,
        out_specs=jax.tree.map(lambda _: VM, outs),
        cost_estimate=pl.CostEstimate(flops=flops, bytes_accessed=nbytes, transcendentals=0),
        compiler_params=pltpu.CompilerParams(vmem_limit_bytes=24 * 2**20),
        name=name,
        **kw,
    )(*args)


def array(shape, dtype):
    return jax.ShapeDtypeStruct(shape, dtype)


def after(value, *tokens):
    return lax.optimization_barrier((value,) + tokens)[0]


def dense_plan(feats, weight, degree, tile_cols, adjacency, cotangent):
    blocks, half, width = feats.shape
    slots = tile_cols.shape[1]
    side = adjacency.shape[2]
    n = lax.axis_size("row")
    rows = blocks * half
    hrows = rows // 2
    span = blocks * side
    far = n // 2
    ring = [2 * p if p < far else 2 * (n - 1 - p) + 1 for p in range(n)]
    fwd = [(ring[p], ring[(p + 1) % n]) for p in range(n)]
    bwd = [(b, a) for a, b in fwd]

    def half_rows_of(d, h):
        me = lax.axis_index("row")
        z = lax.shift_right_logical(me, 1)
        place = jnp.where(lax.rem(me, 2) == 0, z, n - 1 - z)
        p = lax.rem(place + (d + n), n)
        owner = jnp.where(p < far, 2 * p, 2 * (n - 1 - p) + 1)
        return pl.ds(pl.multiple_of(owner * rows + h * hrows, hrows), hrows)

    def item_cost(items):
        return 2 * hrows * span * width * items, items * hrows * span * 2

    def project(deg_hbm, x_hbm, w_hbm, s0, s1, sc, deg, x, w, sems):
        copies = [
            pltpu.make_async_copy(src, dst, sems.at[i])
            for i, (src, dst) in enumerate(((deg_hbm, deg), (x_hbm, x), (w_hbm, w)))
        ]
        for c in copies:
            c.start()
        copies[0].wait()
        scale = lax.rsqrt(deg[...].astype(F32) + 1.0)
        eye = lax.broadcasted_iota(jnp.int32, (half, half), 0) == lax.broadcasted_iota(
            jnp.int32, (half, half), 1
        )
        for b in range(blocks):
            line = jnp.broadcast_to(scale[b : b + 1, :], (half, half))
            col = jnp.sum(jnp.where(eye, line, 0.0), axis=1, keepdims=True)
            sc[b * half : (b + 1) * half, :] = jnp.broadcast_to(col, (half, 128))
        copies[1].wait()
        copies[2].wait()
        proj = jnp.dot(x[...], w[...], preferred_element_type=F32)
        out = (jnp.tile(sc[...], (1, width // 128)) * proj).astype(BF16)
        s0[...] = out[:hrows]
        s1[...] = out[hrows:]

    hshape = (hrows, width)
    s0, s1, scale = call(
        project,
        (array(hshape, BF16), array(hshape, BF16), array((rows, 128), F32)),
        [ANY] * 3,
        tuple(
            pltpu.with_memory_space_constraint(a, pltpu.HBM)
            for a in (degree, feats.reshape(rows, width), weight)
        ),
        2 * rows * width * width,
        2 * rows * width * 2,
        "project",
        scratch_shapes=[
            pltpu.VMEM(degree.shape, jnp.int32),
            pltpu.VMEM((rows, width), BF16),
            pltpu.VMEM(weight.shape, BF16),
            pltpu.SemaphoreType.DMA((3,)),
        ],
    )

    def densify(cols_hbm, adj_hbm, dense, cols, adj, sems):
        def tiles_of(b):
            return pl.ds(b * slots, slots)

        cols_copy = pltpu.make_async_copy(cols_hbm, cols, sems.at[blocks])
        cols_copy.start()
        copies = [
            pltpu.make_async_copy(adj_hbm.at[tiles_of(b)], adj.at[tiles_of(b)], sems.at[b])
            for b in range(blocks)
        ]
        for c in copies:
            c.start()
        dense[...] = jnp.zeros(dense.shape, BF16)
        cols_copy.wait()
        for b in range(blocks):
            copies[b].wait()
            lanes = slice(b * side, (b + 1) * side)
            for k in range(slots):
                c = cols[b, k]
                tile = jnp.where(c >= 0, adj[b * slots + k], 0).astype(F32).astype(BF16)
                place = pl.ds(pl.multiple_of(jnp.maximum(c, 0) * half, half), half)
                dense[place, lanes] = dense[place, lanes] + tile

    def hbm(x):
        return pltpu.with_memory_space_constraint(x, pltpu.HBM)

    dense = pl.pallas_call(
        densify,
        out_shape=pltpu.VMEM((n * rows, span), BF16),
        in_specs=[ANY, ANY],
        out_specs=VM,
        scratch_shapes=[
            pltpu.SMEM(tile_cols.shape, jnp.int32),
            pltpu.VMEM(adjacency.shape, jnp.int32),
            pltpu.SemaphoreType.DMA((blocks + 1,)),
        ],
        cost_estimate=pl.CostEstimate(
            flops=0, bytes_accessed=adjacency.size * 4, transcendentals=0
        ),
        compiler_params=pltpu.CompilerParams(vmem_limit_bytes=24 * 2**20),
        name="densify",
    )(hbm(tile_cols), hbm(adjacency))

    def shift_pair(pair):
        return lax.ppermute(pair[0], "row", fwd), lax.ppermute(pair[1], "row", bwd)

    def gather_terms(dense, items):
        total = None
        for d, h, ref in items:
            term = lax.dot_general(
                ref[...], dense[half_rows_of(d, h), :], (((0,), (0,)), ((), ())),
                preferred_element_type=F32,
            )
            total = term if total is None else total + term
        return total

    def gather(items, part, name):
        def body(dense, *refs):
            total = gather_terms(dense, [(d, h, r) for (d, h, _), r in zip(items, refs)])
            refs[-1][...] = total if part is None else refs[-2][...] + total

        extra = () if part is None else (part,)
        return call(
            body,
            array((width, span), F32),
            [VM] * (1 + len(items) + len(extra)),
            (dense, *[i[2] for i in items], *extra),
            *item_cost(len(items)),
            name,
        )

    long, short = [(s0, s1)], [(s1, s0)]
    long.append(shift_pair(long[0]))
    short.append(shift_pair(short[0]))

    def pass_on(pair, token):
        first = after(pair[0], token)
        return first, after(pair[1], first)

    long[1] = pass_on(long[1], dense)
    long.append(shift_pair(long[1]))
    short[1] = pass_on(short[1], long[1][1])
    short.append(shift_pair(short[1]))

    def long_items(hop):
        return [(-hop, 0, long[hop][0]), (hop, 1, long[hop][1])]

    def short_items(hop):
        return [(-hop, 1, short[hop][0]), (hop, 0, short[hop][1])]

    part = gather([(0, 0, s0), (0, 1, s1)] + long_items(1), None, "gather_near")
    long[2] = pass_on(long[2], part)
    long.append(shift_pair(long[2]))
    part = gather(short_items(1) + long_items(2), part, "gather_two")
    short[2] = pass_on(short[2], part)
    short.append(shift_pair(short[2]))
    long[3] = pass_on(long[3], short[2][1])
    long.append(shift_pair(long[3]))
    part = gather(short_items(2) + long_items(3), part, "gather_three")

    def turn(dense, fa, ba, part, give, keep, tgive, tkeep, dgive, dkeep, whole, wide):
        q = lax.axis_index("col")
        total = part[...] + gather_terms(dense, [(-(far - 1), 1, fa), (far - 1, 0, ba)])
        whole[...] = total.T.reshape(blocks, 2, half, width)
        for h in range(2):
            block = dense[half_rows_of(far, h), :].T
            wide[:, :, :, h * hrows : (h + 1) * hrows] = block.reshape(blocks, 2, half, hrows)
        give[...] = whole[:, 1 - q].reshape(rows, width)
        keep[...] = whole[:, q].reshape(rows, width)
        tg = wide[:, 1 - q].reshape(rows, rows)
        tk = wide[:, q].reshape(rows, rows)
        tgive[...] = tg
        tkeep[...] = tk
        dgive[...] = tg.T
        dkeep[...] = tk.T

    shape = (rows, width)
    square = (rows, rows)
    part_give, part_keep, turn_give, turn_keep, far_give, far_keep = call(
        turn,
        (array(shape, F32), array(shape, F32)) + (array(square, BF16),) * 4,
        [VM] * 4,
        (dense, *short[3], part),
        *item_cost(3),
        "turn",
        scratch_shapes=[
            pltpu.VMEM((blocks, 2, half, width), F32),
            pltpu.VMEM((blocks, 2, half, rows), BF16),
        ],
    )

    def last(part, turned, fa, ba, out):
        total = part[...] + jnp.dot(turned[:, :hrows], fa[...], preferred_element_type=F32)
        total = total + jnp.dot(turned[:, hrows:], ba[...], preferred_element_type=F32)
        out[...] = total.astype(out.dtype)

    def gather_last(part, turned, dtype, name):
        return call(
            last, array(shape, dtype), [VM] * 4, (part, turned, *long[far]), *item_cost(1), name
        )

    give = gather_last(part_give, turn_give, BF16, "gather_give")
    got = lax.ppermute(give, "col", OTHER)
    keep = gather_last(part_keep, turn_keep, F32, "gather_keep")

    def mixed_of(keep, got, s0, s1, sc, h):
        at = slice(h * hrows, (h + 1) * hrows)
        s = jnp.tile(sc[at, :], (1, width // 128))
        sent = (s0, s1)[h][...].astype(F32)
        mixed = s * (keep[at, :] + got[at, :].astype(F32) + sent)
        return at, s, mixed, jax.nn.sigmoid(mixed)

    def mix_back(keep, got, s0, s1, sc, cot, back):
        for h in range(2):
            at, s, mixed, sig = mixed_of(keep, got, s0, s1, sc, h)
            slope = sig * (1.0 + mixed * (1.0 - sig))
            back[at, :] = (s * cot[at, :].astype(F32) * slope).astype(BF16)

    def mix_out(keep, got, s0, s1, sc, out):
        for h in range(2):
            at, _, mixed, sig = mixed_of(keep, got, s0, s1, sc, h)
            out[at, :] = (mixed * sig).astype(BF16)

    mix_in = (keep, got, s0, s1, scale)
    back = call(
        mix_back,
        array(shape, BF16),
        [VM] * 6,
        mix_in + (cotangent.reshape(shape),),
        rows * width * 20,
        rows * width * 16,
        "mix_back",
    )
    peer_back = lax.ppermute(back, "col", OTHER)
    output = call(
        mix_out, array(shape, BF16), [VM] * 5, mix_in, rows * width * 10, rows * width * 12, "mix_out"
    )

    def far_own(matrix, back, out):
        out[...] = jnp.dot(matrix[...], back[...], preferred_element_type=F32)

    far_part = call(
        far_own, array(shape, F32), [VM] * 2, (far_keep, back), *item_cost(1), "return_far_own"
    )

    def far_peer(matrix, back, part, c0, c1):
        out = part[...] + jnp.dot(matrix[...], back[...], preferred_element_type=F32)
        c0[...] = out[:hrows].astype(BF16)
        c1[...] = out[hrows:].astype(BF16)

    up = call(
        far_peer,
        (array(hshape, BF16), array(hshape, BF16)),
        [VM] * 3,
        (far_give, peer_back, far_part),
        *item_cost(1),
        "return_far",
    )
    up = shift_pair(up)

    def chunk(dense, full, d, h):
        return jnp.dot(dense[half_rows_of(d, h), :], full, preferred_element_type=F32)

    def return_next(dense, back, peer, full4, first, second):
        q = lax.axis_index("col")
        full4[:, q] = back[...].reshape(blocks, half, width)
        full4[:, 1 - q] = peer[...].reshape(blocks, half, width)
        full = full4[...].reshape(span, width)
        first[...] = chunk(dense, full, far - 1, 1).astype(BF16)
        second[...] = chunk(dense, full, 1 - far, 0).astype(BF16)

    full4, *down = call(
        return_next,
        (array((blocks, 2, half, width), BF16), array(hshape, BF16), array(hshape, BF16)),
        [VM] * 3,
        (dense, back, peer_back),
        *item_cost(2),
        "return_next",
    )
    full = full4.reshape(span, width)
    down = shift_pair(down)

    def chunks(which, full, name):
        def body(dense, full, *outs):
            for (d, h), out in zip(which, outs):
                out[...] = chunk(dense, full[...], d, h)

        return call(
            body,
            tuple(array(hshape, F32) for _ in which),
            [VM] * 2,
            (dense, full),
            *item_cost(len(which)),
            name,
        )

    def add_pair(pair, terms, token):
        first = (pair[0].astype(F32) + after(terms[0], token)).astype(BF16)
        second = (pair[1].astype(F32) + after(terms[1], first)).astype(BF16)
        return first, second

    a0, a1, c0, c1 = chunks([(3, 0), (-3, 1), (2, 1), (-2, 0)], full, "return_a")
    up = add_pair(up, (a0, a1), c0)
    full_b = after(full, up[1])
    up = shift_pair(up)
    d0, d1, e0, e1 = chunks([(2, 0), (-2, 1), (1, 1), (-1, 0)], full_b, "return_b")
    down = add_pair(down, (c0, c1), d0)
    full_c = after(full, down[1])
    down = shift_pair(down)
    f0, f1, own0, own1 = chunks([(1, 0), (-1, 1), (0, 0), (0, 1)], full_c, "return_c")
    up = add_pair(up, (d0, d1), f0)
    token = up[1]
    up = shift_pair(up)
    down = add_pair(down, (e0, e1), token)
    token = down[1]
    down = shift_pair(down)
    up = shift_pair(add_pair(up, (f0, f1), token))

    def finish(own0, own1, g0, r1, g1, r0, back, sc, w, out):
        for h, (own, g, r) in enumerate(((own0, g0, r0), (own1, g1, r1))):
            at = slice(h * hrows, (h + 1) * hrows)
            total = own[...] + g[...].astype(F32) + r[...].astype(F32)
            s = jnp.tile(sc[at, :], (1, width // 128))
            comb = (s * (total + back[at, :].astype(F32))).astype(BF16)
            out[at, :] = lax.dot_general(
                comb, w[...], (((1,), (1,)), ((), ())), preferred_element_type=F32
            ).astype(BF16)

    grad = call(
        finish,
        array(shape, BF16),
        [VM] * 9,
        (own0, own1, *up, *down, back, scale, weight),
        2 * rows * width * width,
        rows * width * 8,
        "finish",
    )
    return output.reshape(feats.shape), grad.reshape(feats.shape)


def shards(feats, weight, degree, tile_cols, adjacency, cotangent):
    n = lax.axis_size("row")
    blocks, half, width = feats.shape
    dense = (
        n * blocks <= blocks * tile_cols.shape[1]
        and n % 2 == 0
        and n == 8
        and blocks % 2 == 0
        and half % 16 == 0
        and width % 128 == 0
        and adjacency.shape[2] == 2 * half
        and lax.axis_size("col") == 2
    )
    plan = dense_plan if dense else sparse_plan
    return plan(feats, weight, degree, tile_cols, adjacency, cotangent)


def solution(mesh):
    in_specs = (
        P(("grp", "row"), "col", None),
        P(),
        P(("grp", "row"), "col"),
        P(("grp", "row"), None),
        P(("grp", "row"), "col", None),
        P(("grp", "row"), "col", None),
    )
    out_specs = (P(("grp", "row"), "col", None), P(("grp", "row"), "col", None))
    return jax.shard_map(shards, mesh=mesh, in_specs=in_specs, out_specs=out_specs, check_vma=False)
```

```python
import functools

import jax
import jax.numpy as jnp
from jax import lax
from jax.experimental import pallas as pl
from jax.experimental.pallas import tpu as pltpu
from jax.sharding import PartitionSpec as P

F32 = jnp.float32
BF16 = jnp.bfloat16


def sparse_plan(feats, weight, degree, tile_cols, adjacency, cotangent):
    blocks, half_rows, feat_width = feats.shape
    slots_per = tile_cols.shape[1]
    tile_side = adjacency.shape[2]
    peer_count = lax.axis_size("row")
    tile_count = blocks * slots_per
    per_peer = (tile_count + peer_count - 1) // peer_count
    capacity = peer_count * per_peer
    columns = tile_cols.reshape(tile_count)
    is_live = columns >= 0
    owners = jnp.where(is_live, columns // blocks, -1)
    local_block = jnp.where(is_live, columns % blocks, -1)
    earlier = jnp.arange(tile_count)[:, None] > jnp.arange(tile_count)[None, :]
    same_owner = (owners[:, None] == owners[None, :]) & earlier & is_live[None, :]
    tile_rank = jnp.sum(same_owner.astype(jnp.int32), axis=1)
    target_slot = jnp.where(is_live, owners * per_peer + tile_rank, capacity)
    wanted = jnp.zeros((capacity,), jnp.int32).at[target_slot].set(local_block + 1, mode="drop")
    wanted = wanted.reshape(peer_count, per_peer)
    received = lax.all_to_all(wanted, "row", split_axis=0, concat_axis=0, tiled=True)
    incoming = received - 1
    scaling = lax.rsqrt(degree.astype(F32) + 1.0)[..., None]
    projected = jnp.dot(
        feats.reshape(blocks * half_rows, feat_width), weight, preferred_element_type=F32
    )
    sent_rows = (scaling * projected.reshape(blocks, half_rows, feat_width)).astype(BF16)
    tiles_bf = adjacency.astype(BF16).reshape(blocks, slots_per, half_rows, tile_side)
    pick_index = jnp.where(incoming < 0, blocks, incoming)
    replies = jnp.take(sent_rows, pick_index, axis=0, mode="fill", fill_value=0)
    fetched = lax.all_to_all(replies, "row", split_axis=0, concat_axis=0, tiled=True).reshape(
        capacity, half_rows, feat_width
    )
    tile_feats = jnp.take(fetched, target_slot, axis=0, mode="fill", fill_value=0)
    tile_feats = tile_feats.reshape(blocks, slots_per, half_rows, feat_width)
    gathered = lax.dot_general(
        tiles_bf, tile_feats, (((1, 2), (1, 2)), ((0,), (0,))), preferred_element_type=F32
    )
    own_rows = lax.psum_scatter(gathered, "col", scatter_dimension=1, tiled=True)
    mixed = scaling * (own_rows + sent_rows.astype(F32))
    sigmoid_z = jax.nn.sigmoid(mixed)
    output = (mixed * sigmoid_z).astype(BF16)
    silu_slope = sigmoid_z * (1.0 + mixed * (1.0 - sigmoid_z))
    back_sent = (scaling * cotangent.astype(F32) * silu_slope).astype(BF16)
    full_rows = lax.all_gather(back_sent, "col", axis=1, tiled=True)
    partials = lax.dot_general(
        tiles_bf, full_rows, (((3,), (1,)), ((0,), (0,))), preferred_element_type=F32
    )
    outgoing = jnp.zeros((capacity, half_rows, feat_width), F32)
    outgoing = outgoing.at[target_slot].set(
        partials.reshape(tile_count, half_rows, feat_width), mode="drop"
    )
    outgoing = outgoing.reshape(peer_count, per_peer, half_rows, feat_width)
    arrived = lax.all_to_all(outgoing, "row", split_axis=0, concat_axis=0, tiled=True).reshape(
        capacity, half_rows, feat_width
    )
    selector = (incoming.reshape(capacity)[:, None] == jnp.arange(blocks)[None, :]).astype(F32)
    returned = jnp.einsum("sl,sjf->ljf", selector, arrived, precision=lax.Precision.HIGHEST)
    combined = (scaling * (returned + back_sent.astype(F32))).astype(BF16)
    grad_rows = jnp.dot(
        combined.reshape(blocks * half_rows, feat_width), weight.T, preferred_element_type=F32
    )
    return (output, grad_rows.astype(BF16).reshape(blocks, half_rows, feat_width))


VM = pl.BlockSpec(memory_space=pltpu.VMEM)
ANY = pl.BlockSpec(memory_space=pl.ANY)
OTHER = [(0, 1), (1, 0)]


def call(body, outs, ins, args, name, **kw):
    return pl.pallas_call(
        body,
        out_shape=outs,
        in_specs=ins,
        out_specs=jax.tree.map(lambda _: VM, outs),
        cost_estimate=pl.CostEstimate(flops=0, bytes_accessed=0, transcendentals=0),
        compiler_params=pltpu.CompilerParams(vmem_limit_bytes=24 * 2**20),
        name=name,
        **kw,
    )(*args)


def array(shape, dtype):
    return jax.ShapeDtypeStruct(shape, dtype)


def after(value, *tokens):
    return lax.optimization_barrier((value,) + tokens)[0]


def dense_plan(feats, weight, degree, tile_cols, adjacency, cotangent):
    blocks, half, width = feats.shape
    slots = tile_cols.shape[1]
    side = adjacency.shape[2]
    n = lax.axis_size("row")
    rows = blocks * half
    hrows = rows // 2
    span = blocks * side
    far = n // 2
    ring = [2 * p if p < far else 2 * (n - 1 - p) + 1 for p in range(n)]
    fwd = [(ring[p], ring[(p + 1) % n]) for p in range(n)]
    bwd = [(b, a) for a, b in fwd]

    def half_rows_of(d, h):
        me = lax.axis_index("row")
        z = lax.shift_right_logical(me, 1)
        place = jnp.where(lax.rem(me, 2) == 0, z, n - 1 - z)
        p = lax.rem(place + (d + n), n)
        owner = jnp.where(p < far, 2 * p, 2 * (n - 1 - p) + 1)
        return pl.ds(pl.multiple_of(owner * rows + h * hrows, hrows), hrows)

    def scale_columns(degree_values):
        scale = lax.rsqrt(degree_values.astype(F32) + 1.0)
        eye = lax.broadcasted_iota(jnp.int32, (half, half), 0) == lax.broadcasted_iota(
            jnp.int32, (half, half), 1
        )
        for b in range(blocks):
            line = jnp.broadcast_to(scale[b : b + 1, :], (half, half))
            column = jnp.sum(jnp.where(eye, line, 0.0), axis=1, keepdims=True)
            yield b, jnp.broadcast_to(column, (half, 128))

    def over(scale):
        return jnp.tile(scale, (1, width // 128))

    def project(deg_hbm, x_hbm, w_hbm, s0, s1, sc, deg, x, w, sems):
        deg_copy = pltpu.make_async_copy(deg_hbm, deg, sems.at[0])
        deg_copy.start()
        copies = []
        for src, dst, parts in ((x_hbm, x, 4), (w_hbm, w, 2)):
            step = src.shape[0] // parts
            for i in range(parts):
                at = pl.ds(i * step, step)
                copies.append(
                    pltpu.make_async_copy(src.at[at], dst.at[at], sems.at[1 + len(copies)])
                )
                copies[-1].start()
        deg_copy.wait()
        for b, column in scale_columns(deg[...]):
            sc[b * half : (b + 1) * half, :] = column
        for c in copies:
            c.wait()
        proj = jnp.dot(x[...], w[...], preferred_element_type=F32)
        out = (over(sc[...]) * proj).astype(BF16)
        s0[...] = out[:hrows]
        s1[...] = out[hrows:]

    hshape = (hrows, width)
    s0, s1, scale = call(
        project,
        (array(hshape, BF16), array(hshape, BF16), array((rows, 128), F32)),
        [ANY] * 3,
        tuple(
            pltpu.with_memory_space_constraint(a, pltpu.HBM)
            for a in (degree, feats.reshape(rows, width), weight)
        ),
        "project",
        scratch_shapes=[
            pltpu.VMEM(degree.shape, jnp.int32),
            pltpu.VMEM((rows, width), BF16),
            pltpu.VMEM(weight.shape, BF16),
            pltpu.SemaphoreType.DMA((7,)),
        ],
    )

    def densify(cols_hbm, adj_hbm, deg_hbm, cot_hbm, dense, pack, cols, adj, deg, sems):
        def tiles_of(b):
            return pl.ds(b * slots, slots)

        cols_copy = pltpu.make_async_copy(cols_hbm, cols, sems.at[blocks])
        deg_copy = pltpu.make_async_copy(deg_hbm, deg, sems.at[blocks + 1])
        cot_copy = pltpu.make_async_copy(cot_hbm, pack.at[pl.ds(0, rows)], sems.at[blocks + 2])
        cols_copy.start()
        deg_copy.start()
        copies = [
            pltpu.make_async_copy(adj_hbm.at[tiles_of(b)], adj.at[tiles_of(b)], sems.at[b])
            for b in range(blocks)
        ]
        for c in copies:
            c.start()
        cot_copy.start()
        dense[...] = jnp.zeros(dense.shape, BF16)
        pack[rows:, :] = jnp.zeros((16, width), BF16)
        deg_copy.wait()
        padded = jnp.concatenate([deg[...], jnp.zeros((16 - blocks, half), jnp.int32)], axis=0)
        pack[rows:, :half] = padded.astype(F32).astype(BF16)
        cols_copy.wait()
        for b in range(blocks):
            copies[b].wait()
            lanes = slice(b * side, (b + 1) * side)
            for k in range(slots):
                c = cols[b, k]
                tile = jnp.where(c >= 0, adj[b * slots + k], 0).astype(F32).astype(BF16)
                place = pl.ds(pl.multiple_of(jnp.maximum(c, 0) * half, half), half)
                dense[place, lanes] = dense[place, lanes] + tile
        cot_copy.wait()

    def hbm(x):
        return pltpu.with_memory_space_constraint(x, pltpu.HBM)

    shape = (rows, width)
    dense, pack = pl.pallas_call(
        densify,
        out_shape=(pltpu.VMEM((n * rows, span), BF16), array((rows + 16, width), BF16)),
        in_specs=[ANY] * 4,
        out_specs=(VM, VM),
        scratch_shapes=[
            pltpu.SMEM(tile_cols.shape, jnp.int32),
            pltpu.VMEM(adjacency.shape, jnp.int32),
            pltpu.VMEM(degree.shape, jnp.int32),
            pltpu.SemaphoreType.DMA((blocks + 3,)),
        ],
        cost_estimate=pl.CostEstimate(flops=0, bytes_accessed=0, transcendentals=0),
        compiler_params=pltpu.CompilerParams(vmem_limit_bytes=24 * 2**20),
        name="densify",
    )(hbm(tile_cols), hbm(adjacency), hbm(degree), hbm(cotangent.reshape(shape)))

    def shift_pair(pair):
        return lax.ppermute(pair[0], "row", fwd), lax.ppermute(pair[1], "row", bwd)

    def gather_terms(dense, items):
        total = None
        for d, h, ref in items:
            term = lax.dot_general(
                ref[...], dense[half_rows_of(d, h), :], (((0,), (0,)), ((), ())),
                preferred_element_type=F32,
            )
            total = term if total is None else total + term
        return total

    def gather(items, part, name):
        def body(dense, *refs):
            total = gather_terms(dense, [(d, h, r) for (d, h, _), r in zip(items, refs)])
            refs[-1][...] = total if part is None else refs[-2][...] + total

        extra = () if part is None else (part,)
        return call(
            body,
            array((width, span), F32),
            [VM] * (1 + len(items) + len(extra)),
            (dense, *[i[2] for i in items], *extra),
            name,
        )

    long, short = [(s0, s1)], [(s1, s0)]
    long.append(shift_pair(long[0]))
    short.append(shift_pair(short[0]))

    long[1] = tuple(after(x, dense) for x in long[1])
    long.append(shift_pair(long[1]))
    short.append(shift_pair(short[1]))
    long.append(shift_pair(long[2]))
    def long_items(hop):
        return [(-hop, 0, long[hop][0]), (hop, 1, long[hop][1])]

    def short_items(hop):
        return [(-hop, 1, short[hop][0]), (hop, 0, short[hop][1])]

    peer_pack = lax.ppermute(pack, "col", OTHER)

    def prepare(pack, peer_pack, scale, scaled):
        mine = lax.axis_index("col")
        for h, p in ((mine, pack), (1 - mine, peer_pack)):
            degrees = p[rows:, :half].astype(F32)[:blocks]
            for b, column in scale_columns(degrees):
                scale[b, h] = column
                scaled[b, h] = over(column) * p[b * half : (b + 1) * half, :].astype(F32)

    scale_all, scaled_cot = call(
        prepare,
        (array((blocks, 2, half, 128), F32), array((blocks, 2, half, width), F32)),
        [VM] * 2,
        (pack, peer_pack),
        "prepare",
    )
    scale_all = scale_all.reshape(span, 128)
    scaled_cot = scaled_cot.reshape(span, width)

    part = gather([(0, 0, s0), (0, 1, s1)] + long_items(1), None, "gather_near")
    short.append(shift_pair(short[2]))
    part = gather(short_items(1) + long_items(2), part, "gather_two")
    long[3] = (after(long[3][0], part), long[3][1])
    long.append(shift_pair(long[3]))
    part = gather(short_items(2) + long_items(3), after(part, scale_all), "gather_three")

    def turn(dense, fa, ba, part, s0, s1, whole, wide):
        total = part[...] + gather_terms(dense, [(-(far - 1), 1, fa), (far - 1, 0, ba)])
        whole[...] = total.T.reshape(blocks, 2, half, width)
        q = lax.axis_index("col")
        for b in range(blocks):
            at = (b * half) % hrows
            own = s0 if b < blocks // 2 else s1
            whole[b, q] = whole[b, q] + own[at : at + half, :].astype(F32)
        for h in range(2):
            wide[:, h * hrows : (h + 1) * hrows] = dense[half_rows_of(far, h), :].T

    part, turned = call(
        turn,
        (array((blocks, 2, half, width), F32), array((span, rows), BF16)),
        [VM] * 6,
        (dense, *short[3], part, s0, s1),
        "turn",
    )
    part = part.reshape(span, width)

    def node_piece(k):
        return slice(k * rows, (k + 1) * rows)

    def last(k, part, turned, fa, ba, keep, give):
        at = node_piece(k)
        total = part[at, :] + jnp.dot(turned[at, :hrows], fa[...], preferred_element_type=F32)
        total = total + jnp.dot(turned[at, hrows:], ba[...], preferred_element_type=F32)
        keep[...] = total
        give[...] = total.astype(BF16)

    keep, got = [], []
    for k in range(2):
        kept, give = call(
            functools.partial(last, k),
            (array(shape, F32), array(shape, BF16)),
            [VM] * 4,
            (part, turned, *long[far]),
            "gather_last",
        )
        keep.append(kept)
        got.append(lax.ppermute(give, "col", OTHER))

    def mix_back(k, keep, got, scale, scaled, back):
        at = node_piece(k)
        mixed = over(scale[at, :]) * (keep[...] + got[...].astype(F32))
        sig = jax.nn.sigmoid(mixed)
        slope = sig * (1.0 + mixed * (1.0 - sig))
        back[...] = (scaled[at, :] * slope).astype(BF16)

    far_rows = lambda dense, k: dense[pl.ds(half_rows_of(far, 0).start, rows), node_piece(k)]

    def far_first(dense, back, out):
        out[...] = jnp.dot(far_rows(dense, 0), back[...], preferred_element_type=F32)

    def far_second(dense, back, part, c0, c1):
        out = part[...] + jnp.dot(far_rows(dense, 1), back[...], preferred_element_type=F32)
        c0[...] = out[:hrows].astype(BF16)
        c1[...] = out[hrows:].astype(BF16)

    back = []
    for k in range(2):
        back.append(
            call(
                functools.partial(mix_back, k),
                array(shape, BF16),
                [VM] * 4,
                (keep[k], got[k], scale_all, scaled_cot),
                "mix_back",
            )
        )
        if k == 0:
            far_part = call(
                far_first, array(shape, F32), [VM] * 2, (dense, back[0]), "return_far_first"
            )
    up = call(
        far_second,
        (array(hshape, BF16), array(hshape, BF16)),
        [VM] * 3,
        (dense, back[1], far_part),
        "return_far",
    )
    token = up[0]
    up = shift_pair(up)

    def chunk(dense, back, d, h):
        at = half_rows_of(d, h)
        return sum(
            jnp.dot(dense[at, node_piece(k)], back[k][...], preferred_element_type=F32)
            for k in range(2)
        )

    def chunks(which, token, name, dtype=F32):
        def body(dense, *refs):
            for (d, h), out in zip(which, refs[2:]):
                out[...] = chunk(dense, refs[:2], d, h).astype(dtype)

        return call(
            body,
            tuple(array(hshape, dtype) for _ in which),
            [VM] * 3,
            (dense, after(back[0], token), back[1]),
            name,
        )

    def add(total, term, token):
        return (total.astype(F32) + term).astype(BF16)

    def shift(x, h):
        return lax.ppermute(x, "row", (fwd, bwd)[h])

    down = chunks([(far - 1, 1), (1 - far, 0)], token, "return_next", BF16)
    token = down[0]
    down = shift_pair(down)
    a0, a1, c0, c1 = chunks([(3, 0), (-3, 1), (2, 1), (-2, 0)], token, "return_a")
    d0, d1 = chunks([(2, 0), (-2, 1)], a0, "return_b")
    u0 = add(up[0], a0, d0)
    e0, e1 = chunks([(1, 1), (-1, 0)], u0, "return_c")
    u1 = add(up[1], a1, e0)
    f0, f1 = chunks([(1, 0), (-1, 1)], u1, "return_d")
    w0 = add(down[0], c0, f0)

    def own_base(dense, back0, back1, base0, base1):
        q = lax.axis_index("col")
        for h, (back, base) in enumerate(((back0, base0), (back1, base1))):
            mine = back[...].reshape(blocks // 2, 2, half, width)
            mine = jnp.where(q == 0, mine[:, 0], mine[:, 1]).reshape(hshape).astype(F32)
            base[...] = chunk(dense, (back0, back1), 0, h) + mine

    base = call(
        own_base,
        (array(hshape, F32), array(hshape, F32)),
        [VM] * 3,
        (dense, after(back[0], w0), back[1]),
        "own_base",
    )
    w1 = add(down[1], c1, base[0])
    u0, u1, w0, w1 = shift(u0, 0), shift(u1, 1), shift(w0, 0), shift(w1, 1)
    v0 = add(u0, d0, w1)
    v1 = add(u1, d1, v0)
    x0 = add(w0, e0, v1)
    x1 = add(w1, e1, x0)
    u0, u1, w0, w1 = shift(v0, 0), shift(v1, 1), shift(x0, 0), shift(x1, 1)
    v0 = add(u0, f0, x1)
    v1 = add(u1, f1, v0)
    up = (shift(v0, 0), shift(v1, 1))
    down = (w0, w1)

    def mix_out(keep0, keep1, got0, got1, scale, out):
        q = lax.axis_index("col")
        for k, (keep, got) in enumerate(((keep0, got0), (keep1, got1))):
            mixed = over(scale[node_piece(k), :]) * (keep[...] + got[...].astype(F32))
            mixed = mixed.reshape(blocks // 2, 2, half, width)
            mixed = jnp.where(q == 0, mixed[:, 0], mixed[:, 1]).reshape(hshape)
            out[k * hrows : (k + 1) * hrows, :] = (mixed * jax.nn.sigmoid(mixed)).astype(BF16)

    output = call(
        mix_out, array(shape, BF16), [VM] * 5, (*keep, *got, after(scale_all, v1)), "mix_out"
    )

    def finish(base0, base1, g0, r1, g1, r0, sc, w, out_hbm, out, sems):
        copies = []
        step = hrows // 2
        for h, (base, g, r) in enumerate(((base0, g0, r0), (base1, g1, r1))):
            for i in range(2):
                at = slice(i * step, (i + 1) * step)
                whole = slice(h * hrows + i * step, h * hrows + (i + 1) * step)
                total = base[at, :] + g[at, :].astype(F32) + r[at, :].astype(F32)
                comb = (over(sc[whole, :]) * total).astype(BF16)
                out[whole, :] = lax.dot_general(
                    comb, w[...], (((1,), (1,)), ((), ())), preferred_element_type=F32
                ).astype(BF16)
                to = pl.ds(h * hrows + i * step, step)
                copies.append(pltpu.make_async_copy(out.at[to], out_hbm.at[to], sems.at[2 * h + i]))
                copies[-1].start()
        for c in copies:
            c.wait()

    grad = pl.pallas_call(
        finish,
        out_shape=array(shape, BF16),
        in_specs=[VM] * 8,
        out_specs=ANY,
        scratch_shapes=[pltpu.VMEM(shape, BF16), pltpu.SemaphoreType.DMA((4,))],
        cost_estimate=pl.CostEstimate(flops=0, bytes_accessed=0, transcendentals=0),
        compiler_params=pltpu.CompilerParams(vmem_limit_bytes=24 * 2**20),
        name="finish",
    )(*base, *up, *down, scale, weight)
    return output.reshape(feats.shape), grad.reshape(feats.shape)


def shards(feats, weight, degree, tile_cols, adjacency, cotangent):
    n = lax.axis_size("row")
    blocks, half, width = feats.shape
    dense = (
        n * blocks <= blocks * tile_cols.shape[1]
        and n % 2 == 0
        and n == 8
        and blocks % 2 == 0
        and blocks <= 16
        and half % 16 == 0
        and width % 128 == 0
        and adjacency.shape[2] == 2 * half
        and lax.axis_size("col") == 2
    )
    plan = dense_plan if dense else sparse_plan
    return plan(feats, weight, degree, tile_cols, adjacency, cotangent)


def solution(mesh):
    in_specs = (
        P(("grp", "row"), "col", None),
        P(),
        P(("grp", "row"), "col"),
        P(("grp", "row"), None),
        P(("grp", "row"), "col", None),
        P(("grp", "row"), "col", None),
    )
    out_specs = (P(("grp", "row"), "col", None), P(("grp", "row"), "col", None))
    return jax.shard_map(shards, mesh=mesh, in_specs=in_specs, out_specs=out_specs, check_vma=False)
```

```python
import functools

import jax
import jax.numpy as jnp
from jax import lax
from jax.experimental import pallas as pl
from jax.experimental.pallas import tpu as pltpu
from jax.sharding import PartitionSpec as P

F32 = jnp.float32
BF16 = jnp.bfloat16


def sparse_plan(feats, weight, degree, tile_cols, adjacency, cotangent):
    blocks, half_rows, feat_width = feats.shape
    slots_per = tile_cols.shape[1]
    tile_side = adjacency.shape[2]
    peer_count = lax.axis_size("row")
    tile_count = blocks * slots_per
    per_peer = (tile_count + peer_count - 1) // peer_count
    capacity = peer_count * per_peer
    columns = tile_cols.reshape(tile_count)
    is_live = columns >= 0
    owners = jnp.where(is_live, columns // blocks, -1)
    local_block = jnp.where(is_live, columns % blocks, -1)
    earlier = jnp.arange(tile_count)[:, None] > jnp.arange(tile_count)[None, :]
    same_owner = (owners[:, None] == owners[None, :]) & earlier & is_live[None, :]
    tile_rank = jnp.sum(same_owner.astype(jnp.int32), axis=1)
    target_slot = jnp.where(is_live, owners * per_peer + tile_rank, capacity)
    wanted = jnp.zeros((capacity,), jnp.int32).at[target_slot].set(local_block + 1, mode="drop")
    wanted = wanted.reshape(peer_count, per_peer)
    received = lax.all_to_all(wanted, "row", split_axis=0, concat_axis=0, tiled=True)
    incoming = received - 1
    scaling = lax.rsqrt(degree.astype(F32) + 1.0)[..., None]
    projected = jnp.dot(
        feats.reshape(blocks * half_rows, feat_width), weight, preferred_element_type=F32
    )
    sent_rows = (scaling * projected.reshape(blocks, half_rows, feat_width)).astype(BF16)
    tiles_bf = adjacency.astype(BF16).reshape(blocks, slots_per, half_rows, tile_side)
    pick_index = jnp.where(incoming < 0, blocks, incoming)
    replies = jnp.take(sent_rows, pick_index, axis=0, mode="fill", fill_value=0)
    fetched = lax.all_to_all(replies, "row", split_axis=0, concat_axis=0, tiled=True).reshape(
        capacity, half_rows, feat_width
    )
    tile_feats = jnp.take(fetched, target_slot, axis=0, mode="fill", fill_value=0)
    tile_feats = tile_feats.reshape(blocks, slots_per, half_rows, feat_width)
    gathered = lax.dot_general(
        tiles_bf, tile_feats, (((1, 2), (1, 2)), ((0,), (0,))), preferred_element_type=F32
    )
    own_rows = lax.psum_scatter(gathered, "col", scatter_dimension=1, tiled=True)
    mixed = scaling * (own_rows + sent_rows.astype(F32))
    sigmoid_z = jax.nn.sigmoid(mixed)
    output = (mixed * sigmoid_z).astype(BF16)
    silu_slope = sigmoid_z * (1.0 + mixed * (1.0 - sigmoid_z))
    back_sent = (scaling * cotangent.astype(F32) * silu_slope).astype(BF16)
    full_rows = lax.all_gather(back_sent, "col", axis=1, tiled=True)
    partials = lax.dot_general(
        tiles_bf, full_rows, (((3,), (1,)), ((0,), (0,))), preferred_element_type=F32
    )
    outgoing = jnp.zeros((capacity, half_rows, feat_width), F32)
    outgoing = outgoing.at[target_slot].set(
        partials.reshape(tile_count, half_rows, feat_width), mode="drop"
    )
    outgoing = outgoing.reshape(peer_count, per_peer, half_rows, feat_width)
    arrived = lax.all_to_all(outgoing, "row", split_axis=0, concat_axis=0, tiled=True).reshape(
        capacity, half_rows, feat_width
    )
    selector = (incoming.reshape(capacity)[:, None] == jnp.arange(blocks)[None, :]).astype(F32)
    returned = jnp.einsum("sl,sjf->ljf", selector, arrived, precision=lax.Precision.HIGHEST)
    combined = (scaling * (returned + back_sent.astype(F32))).astype(BF16)
    grad_rows = jnp.dot(
        combined.reshape(blocks * half_rows, feat_width), weight.T, preferred_element_type=F32
    )
    return (output, grad_rows.astype(BF16).reshape(blocks, half_rows, feat_width))


VM = pl.BlockSpec(memory_space=pltpu.VMEM)
ANY = pl.BlockSpec(memory_space=pl.ANY)
OTHER = [(0, 1), (1, 0)]


def call(body, outs, ins, args, name, **kw):
    return pl.pallas_call(
        body,
        out_shape=outs,
        in_specs=ins,
        out_specs=jax.tree.map(lambda _: VM, outs),
        cost_estimate=pl.CostEstimate(flops=0, bytes_accessed=0, transcendentals=0),
        compiler_params=pltpu.CompilerParams(vmem_limit_bytes=24 * 2**20),
        name=name,
        **kw,
    )(*args)


def array(shape, dtype):
    return jax.ShapeDtypeStruct(shape, dtype)


def after(value, *tokens):
    return lax.optimization_barrier((value,) + tokens)[0]


def dense_plan(feats, weight, degree, tile_cols, adjacency, cotangent):
    blocks, half, width = feats.shape
    slots = tile_cols.shape[1]
    side = adjacency.shape[2]
    n = lax.axis_size("row")
    rows = blocks * half
    hrows = rows // 2
    span = blocks * side
    far = n // 2
    ring = [2 * p if p < far else 2 * (n - 1 - p) + 1 for p in range(n)]
    fwd = [(ring[p], ring[(p + 1) % n]) for p in range(n)]
    bwd = [(b, a) for a, b in fwd]

    def half_rows_of(d, h):
        me = lax.axis_index("row")
        z = lax.shift_right_logical(me, 1)
        place = jnp.where(lax.rem(me, 2) == 0, z, n - 1 - z)
        p = lax.rem(place + (d + n), n)
        owner = jnp.where(p < far, 2 * p, 2 * (n - 1 - p) + 1)
        return pl.ds(pl.multiple_of(owner * rows + h * hrows, hrows), hrows)

    def scale_columns(degree_values):
        scale = lax.rsqrt(degree_values.astype(F32) + 1.0)
        eye = lax.broadcasted_iota(jnp.int32, (half, half), 0) == lax.broadcasted_iota(
            jnp.int32, (half, half), 1
        )
        for b in range(blocks):
            line = jnp.broadcast_to(scale[b : b + 1, :], (half, half))
            column = jnp.sum(jnp.where(eye, line, 0.0), axis=1, keepdims=True)
            yield b, jnp.broadcast_to(column, (half, 128))

    def over(scale):
        return jnp.tile(scale, (1, width // 128))

    def project(deg_hbm, x_hbm, w_hbm, s0, s1, sc, deg, x, w, sems):
        deg_copy = pltpu.make_async_copy(deg_hbm, deg, sems.at[0])
        deg_copy.start()
        copies = []
        for src, dst, parts in ((x_hbm, x, 4), (w_hbm, w, 2)):
            step = src.shape[0] // parts
            for i in range(parts):
                at = pl.ds(i * step, step)
                copies.append(
                    pltpu.make_async_copy(src.at[at], dst.at[at], sems.at[1 + len(copies)])
                )
                copies[-1].start()
        deg_copy.wait()
        for b, column in scale_columns(deg[...]):
            sc[b * half : (b + 1) * half, :] = column
        for c in copies:
            c.wait()
        proj = jnp.dot(x[...], w[...], preferred_element_type=F32)
        out = (over(sc[...]) * proj).astype(BF16)
        s0[...] = out[:hrows]
        s1[...] = out[hrows:]

    hshape = (hrows, width)
    s0, s1, scale = call(
        project,
        (array(hshape, BF16), array(hshape, BF16), array((rows, 128), F32)),
        [ANY] * 3,
        tuple(
            pltpu.with_memory_space_constraint(a, pltpu.HBM)
            for a in (degree, feats.reshape(rows, width), weight)
        ),
        "project",
        scratch_shapes=[
            pltpu.VMEM(degree.shape, jnp.int32),
            pltpu.VMEM((rows, width), BF16),
            pltpu.VMEM(weight.shape, BF16),
            pltpu.SemaphoreType.DMA((7,)),
        ],
    )

    def densify(cols_hbm, adj_hbm, deg_hbm, cot_hbm, dense, pack, cols, adj, deg, sems):
        def tiles_of(b):
            return pl.ds(b * slots, slots)

        cols_copy = pltpu.make_async_copy(cols_hbm, cols, sems.at[blocks])
        deg_copy = pltpu.make_async_copy(deg_hbm, deg, sems.at[blocks + 1])
        cot_copy = pltpu.make_async_copy(cot_hbm, pack.at[pl.ds(0, rows)], sems.at[blocks + 2])
        cols_copy.start()
        deg_copy.start()
        copies = [
            pltpu.make_async_copy(adj_hbm.at[tiles_of(b)], adj.at[tiles_of(b)], sems.at[b])
            for b in range(blocks)
        ]
        for c in copies:
            c.start()
        cot_copy.start()
        dense[...] = jnp.zeros(dense.shape, BF16)
        pack[rows:, :] = jnp.zeros((16, width), BF16)
        deg_copy.wait()
        padded = jnp.concatenate([deg[...], jnp.zeros((16 - blocks, half), jnp.int32)], axis=0)
        pack[rows:, :half] = padded.astype(F32).astype(BF16)
        cols_copy.wait()
        for b in range(blocks):
            copies[b].wait()
            lanes = slice(b * side, (b + 1) * side)
            for k in range(slots):
                c = cols[b, k]
                tile = jnp.where(c >= 0, adj[b * slots + k], 0).astype(F32).astype(BF16)
                place = pl.ds(pl.multiple_of(jnp.maximum(c, 0) * half, half), half)
                dense[place, lanes] = dense[place, lanes] + tile
        cot_copy.wait()

    def hbm(x):
        return pltpu.with_memory_space_constraint(x, pltpu.HBM)

    shape = (rows, width)
    dense, pack = pl.pallas_call(
        densify,
        out_shape=(pltpu.VMEM((n * rows, span), BF16), array((rows + 16, width), BF16)),
        in_specs=[ANY] * 4,
        out_specs=(VM, VM),
        scratch_shapes=[
            pltpu.SMEM(tile_cols.shape, jnp.int32),
            pltpu.VMEM(adjacency.shape, jnp.int32),
            pltpu.VMEM(degree.shape, jnp.int32),
            pltpu.SemaphoreType.DMA((blocks + 3,)),
        ],
        cost_estimate=pl.CostEstimate(flops=0, bytes_accessed=0, transcendentals=0),
        compiler_params=pltpu.CompilerParams(vmem_limit_bytes=24 * 2**20),
        name="densify",
    )(hbm(tile_cols), hbm(adjacency), hbm(degree), hbm(cotangent.reshape(shape)))

    def shift_pair(pair):
        return lax.ppermute(pair[0], "row", fwd), lax.ppermute(pair[1], "row", bwd)

    def gather_terms(dense, items):
        total = None
        for d, h, ref in items:
            term = lax.dot_general(
                ref[...], dense[half_rows_of(d, h), :], (((0,), (0,)), ((), ())),
                preferred_element_type=F32,
            )
            total = term if total is None else total + term
        return total

    def gather(items, part, name):
        def body(dense, *refs):
            total = gather_terms(dense, [(d, h, r) for (d, h, _), r in zip(items, refs)])
            refs[-1][...] = total if part is None else refs[-2][...] + total

        extra = () if part is None else (part,)
        return call(
            body,
            array((width, span), F32),
            [VM] * (1 + len(items) + len(extra)),
            (dense, *[i[2] for i in items], *extra),
            name,
        )

    long, short = [(s0, s1)], [(s1, s0)]
    long.append(shift_pair(long[0]))
    short.append(shift_pair(short[0]))

    long[1] = (after(long[1][0], dense), after(long[1][1], dense))
    long.append(shift_pair(long[1]))
    short.append(shift_pair(short[1]))
    long.append(shift_pair(long[2]))
    def long_items(hop):
        return [(-hop, 0, long[hop][0]), (hop, 1, long[hop][1])]

    def short_items(hop):
        return [(-hop, 1, short[hop][0]), (hop, 0, short[hop][1])]

    peer_pack = lax.ppermute(pack, "col", OTHER)

    def prepare(pack, peer_pack, scale, scaled):
        mine = lax.axis_index("col")
        for h, p in ((mine, pack), (1 - mine, peer_pack)):
            degrees = p[rows:, :half].astype(F32)[:blocks]
            for b, column in scale_columns(degrees):
                scale[b, h] = column
                scaled[b, h] = over(column) * p[b * half : (b + 1) * half, :].astype(F32)

    scale_all, scaled_cot = call(
        prepare,
        (array((blocks, 2, half, 128), F32), array((blocks, 2, half, width), F32)),
        [VM] * 2,
        (pack, peer_pack),
        "prepare",
    )
    scale_all = scale_all.reshape(span, 128)
    scaled_cot = scaled_cot.reshape(span, width)

    part = gather([(0, 0, s0), (0, 1, s1)] + long_items(1), None, "gather_near")
    short.append(shift_pair(short[2]))
    long[3] = (after(long[3][0], part), long[3][1])
    part = gather(short_items(1) + long_items(2), part, "gather_two")
    long[3] = (long[3][0], after(long[3][1], part))
    long.append(shift_pair(long[3]))
    part = gather(short_items(2) + long_items(3), after(part, scale_all), "gather_three")

    def turn(dense, fa, ba, part, s0, s1, whole, wide):
        total = part[...] + gather_terms(dense, [(-(far - 1), 1, fa), (far - 1, 0, ba)])
        whole[...] = total.T.reshape(blocks, 2, half, width)
        q = lax.axis_index("col")
        for b in range(blocks):
            at = (b * half) % hrows
            own = s0 if b < blocks // 2 else s1
            whole[b, q] = whole[b, q] + own[at : at + half, :].astype(F32)
        for h in range(2):
            wide[:, h * hrows : (h + 1) * hrows] = dense[half_rows_of(far, h), :].T

    part, turned = call(
        turn,
        (array((blocks, 2, half, width), F32), array((span, rows), BF16)),
        [VM] * 6,
        (dense, *short[3], part, s0, s1),
        "turn",
    )
    part = part.reshape(span, width)

    def node_piece(k):
        return slice(k * rows, (k + 1) * rows)

    def last(k, part, turned, fa, ba, keep, give):
        at = node_piece(k)
        total = part[at, :] + jnp.dot(turned[at, :hrows], fa[...], preferred_element_type=F32)
        total = total + jnp.dot(turned[at, hrows:], ba[...], preferred_element_type=F32)
        keep[...] = total
        give[...] = total.astype(BF16)

    keep, got = [], []
    for k in range(2):
        kept, give = call(
            functools.partial(last, k),
            (array(shape, F32), array(shape, BF16)),
            [VM] * 4,
            (part, turned, *long[far]),
            "gather_last",
        )
        keep.append(kept)
        got.append(lax.ppermute(give, "col", OTHER))

    def mix_back(k, keep, got, scale, scaled, back):
        at = node_piece(k)
        mixed = over(scale[at, :]) * (keep[...] + got[...].astype(F32))
        sig = jax.nn.sigmoid(mixed)
        slope = sig * (1.0 + mixed * (1.0 - sig))
        back[...] = (scaled[at, :] * slope).astype(BF16)

    far_rows = lambda dense, k: dense[pl.ds(half_rows_of(far, 0).start, rows), node_piece(k)]

    def far_first(dense, back, out):
        out[...] = jnp.dot(far_rows(dense, 0), back[...], preferred_element_type=F32)

    def far_second(dense, back, part, c0, c1):
        out = part[...] + jnp.dot(far_rows(dense, 1), back[...], preferred_element_type=F32)
        c0[...] = out[:hrows].astype(BF16)
        c1[...] = out[hrows:].astype(BF16)

    back = []
    for k in range(2):
        back.append(
            call(
                functools.partial(mix_back, k),
                array(shape, BF16),
                [VM] * 4,
                (keep[k], got[k], scale_all, scaled_cot),
                "mix_back",
            )
        )
        if k == 0:
            far_part = call(
                far_first, array(shape, F32), [VM] * 2, (dense, back[0]), "return_far_first"
            )
    up = call(
        far_second,
        (array(hshape, BF16), array(hshape, BF16)),
        [VM] * 3,
        (dense, back[1], far_part),
        "return_far",
    )
    token = up[0]
    up = shift_pair(up)

    def chunk(dense, back, d, h):
        at = half_rows_of(d, h)
        return sum(
            jnp.dot(dense[at, node_piece(k)], back[k][...], preferred_element_type=F32)
            for k in range(2)
        )

    def chunks(which, token, name, dtype=F32):
        def body(dense, *refs):
            for (d, h), out in zip(which, refs[2:]):
                out[...] = chunk(dense, refs[:2], d, h).astype(dtype)

        return call(
            body,
            tuple(array(hshape, dtype) for _ in which),
            [VM] * 3,
            (dense, after(back[0], token), back[1]),
            name,
        )

    def add(total, term, token):
        return (total.astype(F32) + term).astype(BF16)

    def shift(x, h):
        return lax.ppermute(x, "row", (fwd, bwd)[h])

    down = chunks([(far - 1, 1), (1 - far, 0)], token, "return_next", BF16)
    token = down[0]
    down = shift_pair(down)
    a0, a1, c0, c1 = chunks([(3, 0), (-3, 1), (2, 1), (-2, 0)], token, "return_a")
    d0, d1 = chunks([(2, 0), (-2, 1)], a0, "return_b")
    u0 = (up[0].astype(F32) + a0).astype(BF16)
    e0, e1 = chunks([(1, 1), (-1, 0)], u0, "return_c")
    u1 = (up[1].astype(F32) + a1).astype(BF16)
    f0, f1 = chunks([(1, 0), (-1, 1)], u1, "return_d")
    w0 = (down[0].astype(F32) + c0).astype(BF16)
    def own_base(dense, back0, back1, base0, base1):
        q = lax.axis_index("col")
        for h, (back, base) in enumerate(((back0, base0), (back1, base1))):
            mine = back[...].reshape(blocks // 2, 2, half, width)
            mine = jnp.where(q == 0, mine[:, 0], mine[:, 1]).reshape(hshape).astype(F32)
            base[...] = chunk(dense, (back0, back1), 0, h) + mine

    base = call(
        own_base,
        (array(hshape, F32), array(hshape, F32)),
        [VM] * 3,
        (dense, after(back[0], w0), back[1]),
        "own_base",
    )
    w1 = (down[1].astype(F32) + c1).astype(BF16)
    u0, u1, w0, w1 = shift(u0, 0), shift(u1, 1), shift(w0, 0), shift(w1, 1)
    v0 = (u0.astype(F32) + d0).astype(BF16)
    v1 = (u1.astype(F32) + d1).astype(BF16)
    x0 = (w0.astype(F32) + e0).astype(BF16)
    x1 = (w1.astype(F32) + after(e1, x0)).astype(BF16)
    u0, u1, w0, w1 = shift(v0, 0), shift(v1, 1), shift(x0, 0), shift(x1, 1)
    v0 = (u0.astype(F32) + f0).astype(BF16)
    v1 = (u1.astype(F32) + f1).astype(BF16)
    up = (shift(v0, 0), shift(v1, 1))
    down = (w0, w1)

    def mix_out(keep0, keep1, got0, got1, scale, out):
        q = lax.axis_index("col")
        for k, (keep, got) in enumerate(((keep0, got0), (keep1, got1))):
            mixed = over(scale[node_piece(k), :]) * (keep[...] + got[...].astype(F32))
            mixed = mixed.reshape(blocks // 2, 2, half, width)
            mixed = jnp.where(q == 0, mixed[:, 0], mixed[:, 1]).reshape(hshape)
            out[k * hrows : (k + 1) * hrows, :] = (mixed * jax.nn.sigmoid(mixed)).astype(BF16)

    output = call(
        mix_out, array(shape, BF16), [VM] * 5, (*keep, *got, after(scale_all, v1)), "mix_out"
    )

    def finish(base0, base1, g0, r1, g1, r0, sc, w, out_hbm, out, sems):
        copies = []
        step = hrows // 2
        for h, (base, g, r) in enumerate(((base0, g0, r0), (base1, g1, r1))):
            for i in range(2):
                at = slice(i * step, (i + 1) * step)
                whole = slice(h * hrows + i * step, h * hrows + (i + 1) * step)
                total = base[at, :] + g[at, :].astype(F32) + r[at, :].astype(F32)
                comb = (over(sc[whole, :]) * total).astype(BF16)
                out[whole, :] = lax.dot_general(
                    comb, w[...], (((1,), (1,)), ((), ())), preferred_element_type=F32
                ).astype(BF16)
                to = pl.ds(h * hrows + i * step, step)
                copies.append(pltpu.make_async_copy(out.at[to], out_hbm.at[to], sems.at[2 * h + i]))
                copies[-1].start()
        for c in copies:
            c.wait()

    grad = pl.pallas_call(
        finish,
        out_shape=array(shape, BF16),
        in_specs=[VM] * 8,
        out_specs=ANY,
        scratch_shapes=[pltpu.VMEM(shape, BF16), pltpu.SemaphoreType.DMA((4,))],
        cost_estimate=pl.CostEstimate(flops=0, bytes_accessed=0, transcendentals=0),
        compiler_params=pltpu.CompilerParams(vmem_limit_bytes=24 * 2**20),
        name="finish",
    )(*base, *up, *down, scale, weight)
    return output.reshape(feats.shape), grad.reshape(feats.shape)


def shards(feats, weight, degree, tile_cols, adjacency, cotangent):
    n = lax.axis_size("row")
    blocks, half, width = feats.shape
    dense = (
        n * blocks <= blocks * tile_cols.shape[1]
        and n % 2 == 0
        and n == 8
        and blocks % 2 == 0
        and blocks <= 16
        and half % 16 == 0
        and width % 128 == 0
        and adjacency.shape[2] == 2 * half
        and lax.axis_size("col") == 2
    )
    plan = dense_plan if dense else sparse_plan
    return plan(feats, weight, degree, tile_cols, adjacency, cotangent)


def solution(mesh):
    in_specs = (
        P(("grp", "row"), "col", None),
        P(),
        P(("grp", "row"), "col"),
        P(("grp", "row"), None),
        P(("grp", "row"), "col", None),
        P(("grp", "row"), "col", None),
    )
    out_specs = (P(("grp", "row"), "col", None), P(("grp", "row"), "col", None))
    return jax.shard_map(shards, mesh=mesh, in_specs=in_specs, out_specs=out_specs, check_vma=False)
```

```python
import functools

import jax
import jax.numpy as jnp
from jax import lax
from jax.experimental import pallas as pl
from jax.experimental.pallas import tpu as pltpu
from jax.sharding import PartitionSpec as P

F32 = jnp.float32
BF16 = jnp.bfloat16


def sparse_plan(feats, weight, degree, tile_cols, adjacency, cotangent):
    blocks, half_rows, feat_width = feats.shape
    slots_per = tile_cols.shape[1]
    tile_side = adjacency.shape[2]
    peer_count = lax.axis_size("row")
    tile_count = blocks * slots_per
    per_peer = (tile_count + peer_count - 1) // peer_count
    capacity = peer_count * per_peer
    columns = tile_cols.reshape(tile_count)
    is_live = columns >= 0
    owners = jnp.where(is_live, columns // blocks, -1)
    local_block = jnp.where(is_live, columns % blocks, -1)
    earlier = jnp.arange(tile_count)[:, None] > jnp.arange(tile_count)[None, :]
    same_owner = (owners[:, None] == owners[None, :]) & earlier & is_live[None, :]
    tile_rank = jnp.sum(same_owner.astype(jnp.int32), axis=1)
    target_slot = jnp.where(is_live, owners * per_peer + tile_rank, capacity)
    wanted = jnp.zeros((capacity,), jnp.int32).at[target_slot].set(local_block + 1, mode="drop")
    wanted = wanted.reshape(peer_count, per_peer)
    received = lax.all_to_all(wanted, "row", split_axis=0, concat_axis=0, tiled=True)
    incoming = received - 1
    scaling = lax.rsqrt(degree.astype(F32) + 1.0)[..., None]
    projected = jnp.dot(
        feats.reshape(blocks * half_rows, feat_width), weight, preferred_element_type=F32
    )
    sent_rows = (scaling * projected.reshape(blocks, half_rows, feat_width)).astype(BF16)
    tiles_bf = adjacency.astype(BF16).reshape(blocks, slots_per, half_rows, tile_side)
    pick_index = jnp.where(incoming < 0, blocks, incoming)
    replies = jnp.take(sent_rows, pick_index, axis=0, mode="fill", fill_value=0)
    fetched = lax.all_to_all(replies, "row", split_axis=0, concat_axis=0, tiled=True).reshape(
        capacity, half_rows, feat_width
    )
    tile_feats = jnp.take(fetched, target_slot, axis=0, mode="fill", fill_value=0)
    tile_feats = tile_feats.reshape(blocks, slots_per, half_rows, feat_width)
    gathered = lax.dot_general(
        tiles_bf, tile_feats, (((1, 2), (1, 2)), ((0,), (0,))), preferred_element_type=F32
    )
    own_rows = lax.psum_scatter(gathered, "col", scatter_dimension=1, tiled=True)
    mixed = scaling * (own_rows + sent_rows.astype(F32))
    sigmoid_z = jax.nn.sigmoid(mixed)
    output = (mixed * sigmoid_z).astype(BF16)
    silu_slope = sigmoid_z * (1.0 + mixed * (1.0 - sigmoid_z))
    back_sent = (scaling * cotangent.astype(F32) * silu_slope).astype(BF16)
    full_rows = lax.all_gather(back_sent, "col", axis=1, tiled=True)
    partials = lax.dot_general(
        tiles_bf, full_rows, (((3,), (1,)), ((0,), (0,))), preferred_element_type=F32
    )
    outgoing = jnp.zeros((capacity, half_rows, feat_width), F32)
    outgoing = outgoing.at[target_slot].set(
        partials.reshape(tile_count, half_rows, feat_width), mode="drop"
    )
    outgoing = outgoing.reshape(peer_count, per_peer, half_rows, feat_width)
    arrived = lax.all_to_all(outgoing, "row", split_axis=0, concat_axis=0, tiled=True).reshape(
        capacity, half_rows, feat_width
    )
    selector = (incoming.reshape(capacity)[:, None] == jnp.arange(blocks)[None, :]).astype(F32)
    returned = jnp.einsum("sl,sjf->ljf", selector, arrived, precision=lax.Precision.HIGHEST)
    combined = (scaling * (returned + back_sent.astype(F32))).astype(BF16)
    grad_rows = jnp.dot(
        combined.reshape(blocks * half_rows, feat_width), weight.T, preferred_element_type=F32
    )
    return (output, grad_rows.astype(BF16).reshape(blocks, half_rows, feat_width))


VM = pl.BlockSpec(memory_space=pltpu.VMEM)
ANY = pl.BlockSpec(memory_space=pl.ANY)
OTHER = [(0, 1), (1, 0)]


def call(body, outs, ins, args, name, **kw):
    return pl.pallas_call(
        body,
        out_shape=outs,
        in_specs=ins,
        out_specs=jax.tree.map(lambda _: VM, outs),
        cost_estimate=pl.CostEstimate(flops=0, bytes_accessed=0, transcendentals=0),
        compiler_params=pltpu.CompilerParams(vmem_limit_bytes=24 * 2**20),
        name=name,
        **kw,
    )(*args)


def array(shape, dtype):
    return jax.ShapeDtypeStruct(shape, dtype)


def after(value, *tokens):
    return lax.optimization_barrier((value,) + tokens)[0]


def dense_plan(feats, weight, degree, tile_cols, adjacency, cotangent):
    blocks, half, width = feats.shape
    slots = tile_cols.shape[1]
    side = adjacency.shape[2]
    n = lax.axis_size("row")
    rows = blocks * half
    hrows = rows // 2
    span = blocks * side
    far = n // 2
    ring = [2 * p if p < far else 2 * (n - 1 - p) + 1 for p in range(n)]
    fwd = [(ring[p], ring[(p + 1) % n]) for p in range(n)]
    bwd = [(b, a) for a, b in fwd]

    def half_rows_of(d, h):
        me = lax.axis_index("row")
        z = lax.shift_right_logical(me, 1)
        place = jnp.where(lax.rem(me, 2) == 0, z, n - 1 - z)
        p = lax.rem(place + (d + n), n)
        owner = jnp.where(p < far, 2 * p, 2 * (n - 1 - p) + 1)
        return pl.ds(pl.multiple_of(owner * rows + h * hrows, hrows), hrows)

    def scale_columns(degree_values):
        scale = lax.rsqrt(degree_values.astype(F32) + 1.0)
        eye = lax.broadcasted_iota(jnp.int32, (half, half), 0) == lax.broadcasted_iota(
            jnp.int32, (half, half), 1
        )
        for b in range(blocks):
            line = jnp.broadcast_to(scale[b : b + 1, :], (half, half))
            column = jnp.sum(jnp.where(eye, line, 0.0), axis=1, keepdims=True)
            yield b, jnp.broadcast_to(column, (half, 128))

    def over(scale):
        return jnp.tile(scale, (1, width // 128))

    def project(deg_hbm, x_hbm, w_hbm, s0, s1, sc, deg, x, w, sems):
        deg_copy = pltpu.make_async_copy(deg_hbm, deg, sems.at[0])
        deg_copy.start()
        copies = []
        for src, dst, parts in ((x_hbm, x, 4), (w_hbm, w, 2)):
            step = src.shape[0] // parts
            for i in range(parts):
                at = pl.ds(i * step, step)
                copies.append(
                    pltpu.make_async_copy(src.at[at], dst.at[at], sems.at[1 + len(copies)])
                )
                copies[-1].start()
        deg_copy.wait()
        for b, column in scale_columns(deg[...]):
            sc[b * half : (b + 1) * half, :] = column
        for c in copies:
            c.wait()
        proj = jnp.dot(x[...], w[...], preferred_element_type=F32)
        out = (over(sc[...]) * proj).astype(BF16)
        s0[...] = out[:hrows]
        s1[...] = out[hrows:]

    hshape = (hrows, width)
    s0, s1, scale = call(
        project,
        (array(hshape, BF16), array(hshape, BF16), array((rows, 128), F32)),
        [ANY] * 3,
        tuple(
            pltpu.with_memory_space_constraint(a, pltpu.HBM)
            for a in (degree, feats.reshape(rows, width), weight)
        ),
        "project",
        scratch_shapes=[
            pltpu.VMEM(degree.shape, jnp.int32),
            pltpu.VMEM((rows, width), BF16),
            pltpu.VMEM(weight.shape, BF16),
            pltpu.SemaphoreType.DMA((7,)),
        ],
    )

    def densify(cols_hbm, adj_hbm, deg_hbm, cot_hbm, dense, pack, cols, adj, deg, sems):
        def tiles_of(b):
            return pl.ds(b * slots, slots)

        cols_copy = pltpu.make_async_copy(cols_hbm, cols, sems.at[blocks])
        deg_copy = pltpu.make_async_copy(deg_hbm, deg, sems.at[blocks + 1])
        cot_copy = pltpu.make_async_copy(cot_hbm, pack.at[pl.ds(0, rows)], sems.at[blocks + 2])
        cols_copy.start()
        deg_copy.start()
        copies = [
            pltpu.make_async_copy(adj_hbm.at[tiles_of(b)], adj.at[tiles_of(b)], sems.at[b])
            for b in range(blocks)
        ]
        for c in copies:
            c.start()
        cot_copy.start()
        dense[...] = jnp.zeros(dense.shape, BF16)
        pack[rows:, :] = jnp.zeros((16, width), BF16)
        deg_copy.wait()
        padded = jnp.concatenate([deg[...], jnp.zeros((16 - blocks, half), jnp.int32)], axis=0)
        pack[rows:, :half] = padded.astype(F32).astype(BF16)
        cols_copy.wait()
        for b in range(blocks):
            copies[b].wait()
            lanes = slice(b * side, (b + 1) * side)
            for k in range(slots):
                c = cols[b, k]
                tile = jnp.where(c >= 0, adj[b * slots + k], 0).astype(F32).astype(BF16)
                place = pl.ds(pl.multiple_of(jnp.maximum(c, 0) * half, half), half)
                dense[place, lanes] = dense[place, lanes] + tile
        cot_copy.wait()

    def hbm(x):
        return pltpu.with_memory_space_constraint(x, pltpu.HBM)

    shape = (rows, width)
    dense, pack = pl.pallas_call(
        densify,
        out_shape=(pltpu.VMEM((n * rows, span), BF16), array((rows + 16, width), BF16)),
        in_specs=[ANY] * 4,
        out_specs=(VM, VM),
        scratch_shapes=[
            pltpu.SMEM(tile_cols.shape, jnp.int32),
            pltpu.VMEM(adjacency.shape, jnp.int32),
            pltpu.VMEM(degree.shape, jnp.int32),
            pltpu.SemaphoreType.DMA((blocks + 3,)),
        ],
        cost_estimate=pl.CostEstimate(flops=0, bytes_accessed=0, transcendentals=0),
        compiler_params=pltpu.CompilerParams(vmem_limit_bytes=24 * 2**20),
        name="densify",
    )(hbm(tile_cols), hbm(adjacency), hbm(degree), hbm(cotangent.reshape(shape)))

    def shift_pair(pair):
        return lax.ppermute(pair[0], "row", fwd), lax.ppermute(pair[1], "row", bwd)

    def gather_terms(dense, items):
        total = None
        for d, h, ref in items:
            term = lax.dot_general(
                ref[...], dense[half_rows_of(d, h), :], (((0,), (0,)), ((), ())),
                preferred_element_type=F32,
            )
            total = term if total is None else total + term
        return total

    def gather(items, part, name):
        def body(dense, *refs):
            total = gather_terms(dense, [(d, h, r) for (d, h, _), r in zip(items, refs)])
            refs[-1][...] = total if part is None else refs[-2][...] + total

        extra = () if part is None else (part,)
        return call(
            body,
            array((width, span), F32),
            [VM] * (1 + len(items) + len(extra)),
            (dense, *[i[2] for i in items], *extra),
            name,
        )

    long, short = [(s0, s1)], [(s1, s0)]
    long.append(shift_pair(long[0]))
    short.append(shift_pair(short[0]))

    long[1] = (after(long[1][0], dense), after(long[1][1], dense))
    long.append(shift_pair(long[1]))
    short.append(shift_pair(short[1]))
    long.append(shift_pair(long[2]))
    def long_items(hop):
        return [(-hop, 0, long[hop][0]), (hop, 1, long[hop][1])]

    def short_items(hop):
        return [(-hop, 1, short[hop][0]), (hop, 0, short[hop][1])]

    peer_pack = lax.ppermute(pack, "col", OTHER)

    def prepare(pack, peer_pack, scale, scaled):
        mine = lax.axis_index("col")
        for h, p in ((mine, pack), (1 - mine, peer_pack)):
            degrees = p[rows:, :half].astype(F32)[:blocks]
            for b, column in scale_columns(degrees):
                scale[b, h] = column
                scaled[b, h] = over(column) * p[b * half : (b + 1) * half, :].astype(F32)

    scale_all, scaled_cot = call(
        prepare,
        (array((blocks, 2, half, 128), F32), array((blocks, 2, half, width), F32)),
        [VM] * 2,
        (pack, peer_pack),
        "prepare",
    )
    scale_all = scale_all.reshape(span, 128)
    scaled_cot = scaled_cot.reshape(span, width)

    part = gather([(0, 0, s0), (0, 1, s1)] + long_items(1), None, "gather_near")
    short.append(shift_pair(short[2]))
    long[3] = (after(long[3][0], part), long[3][1])
    part = gather(short_items(1) + long_items(2), part, "gather_two")
    long[3] = (long[3][0], after(long[3][1], part))
    long.append(shift_pair(long[3]))
    part = gather(short_items(2) + long_items(3), after(part, scale_all), "gather_three")

    def turn(dense, fa, ba, part, s0, s1, whole, wide):
        total = part[...] + gather_terms(dense, [(-(far - 1), 1, fa), (far - 1, 0, ba)])
        whole[...] = total.T.reshape(blocks, 2, half, width)
        q = lax.axis_index("col")
        for b in range(blocks):
            at = (b * half) % hrows
            own = s0 if b < blocks // 2 else s1
            whole[b, q] = whole[b, q] + own[at : at + half, :].astype(F32)
        for h in range(2):
            wide[:, h * hrows : (h + 1) * hrows] = dense[half_rows_of(far, h), :].T

    part, turned = call(
        turn,
        (array((blocks, 2, half, width), F32), array((span, rows), BF16)),
        [VM] * 6,
        (dense, *short[3], part, s0, s1),
        "turn",
    )
    part = part.reshape(span, width)

    def node_piece(k):
        return slice(k * rows, (k + 1) * rows)

    def last(k, part, turned, fa, ba, keep, give):
        at = node_piece(k)
        total = part[at, :] + jnp.dot(turned[at, :hrows], fa[...], preferred_element_type=F32)
        total = total + jnp.dot(turned[at, hrows:], ba[...], preferred_element_type=F32)
        keep[...] = total
        give[...] = total.astype(BF16)

    keep, got = [], []
    for k in range(2):
        kept, give = call(
            functools.partial(last, k),
            (array(shape, F32), array(shape, BF16)),
            [VM] * 4,
            (part, turned, *long[far]),
            "gather_last",
        )
        keep.append(kept)
        got.append(lax.ppermute(give, "col", OTHER))

    def back_of(k, keep, got, scale, scaled):
        at = node_piece(k)
        mixed = over(scale[at, :]) * (keep[...] + got[...].astype(F32))
        sig = jax.nn.sigmoid(mixed)
        slope = sig * (1.0 + mixed * (1.0 - sig))
        return (scaled[at, :] * slope).astype(BF16)

    def far_term(k, dense, back):
        at = pl.ds(half_rows_of(far, 0).start, rows)
        return jnp.dot(dense[at, node_piece(k)], back, preferred_element_type=F32)

    def mix_first(keep, got, scale, scaled, dense, back, far_part):
        value = back_of(0, keep, got, scale, scaled)
        back[...] = value
        far_part[...] = far_term(0, dense, value)

    def mix_second(keep, got, scale, scaled, dense, far_part, back, c0, c1):
        value = back_of(1, keep, got, scale, scaled)
        back[...] = value
        out = far_part[...] + far_term(1, dense, value)
        c0[...] = out[:hrows].astype(BF16)
        c1[...] = out[hrows:].astype(BF16)

    back0, far_part = call(
        mix_first,
        (array(shape, BF16), array(shape, F32)),
        [VM] * 5,
        (keep[0], got[0], scale_all, scaled_cot, dense),
        "mix_first",
    )
    back1, *up = call(
        mix_second,
        (array(shape, BF16), array(hshape, BF16), array(hshape, BF16)),
        [VM] * 6,
        (keep[1], got[1], scale_all, scaled_cot, dense, far_part),
        "mix_second",
    )
    back = [back0, back1]
    token = up[0]
    up = shift_pair(up)

    def chunk(dense, back, d, h):
        at = half_rows_of(d, h)
        return sum(
            jnp.dot(dense[at, node_piece(k)], back[k][...], preferred_element_type=F32)
            for k in range(2)
        )

    def chunks(which, token, name, dtype=F32):
        def body(dense, *refs):
            for (d, h), out in zip(which, refs[2:]):
                out[...] = chunk(dense, refs[:2], d, h).astype(dtype)

        return call(
            body,
            tuple(array(hshape, dtype) for _ in which),
            [VM] * 3,
            (dense, after(back[0], token), back[1]),
            name,
        )

    def add(total, term, token):
        return (total.astype(F32) + term).astype(BF16)

    def shift(x, h):
        return lax.ppermute(x, "row", (fwd, bwd)[h])

    down = chunks([(far - 1, 1), (1 - far, 0)], token, "return_next", BF16)
    token = down[0]
    down = shift_pair(down)
    a0, a1, c0, c1, d0, d1 = chunks([(3, 0), (-3, 1), (2, 1), (-2, 0), (2, 0), (-2, 1)], token, "return_ab")
    u0 = (up[0].astype(F32) + a0).astype(BF16)
    u1 = (up[1].astype(F32) + a1).astype(BF16)
    w0 = (down[0].astype(F32) + after(c0, u0, u1)).astype(BF16)
    def own_base(dense, back0, back1, base0, base1):
        q = lax.axis_index("col")
        for h, (back, base) in enumerate(((back0, base0), (back1, base1))):
            mine = back[...].reshape(blocks // 2, 2, half, width)
            mine = jnp.where(q == 0, mine[:, 0], mine[:, 1]).reshape(hshape).astype(F32)
            base[...] = chunk(dense, (back0, back1), 0, h) + mine

    base = call(
        own_base,
        (array(hshape, F32), array(hshape, F32)),
        [VM] * 3,
        (dense, after(back[0], w0), back[1]),
        "own_base",
    )
    w1 = (down[1].astype(F32) + c1).astype(BF16)
    u0, u1, w0, w1 = shift(u0, 0), shift(u1, 1), shift(w0, 0), shift(w1, 1)
    v0 = (u0.astype(F32) + d0).astype(BF16)
    v1 = (u1.astype(F32) + d1).astype(BF16)
    e0, e1 = chunks([(1, 1), (-1, 0)], v0, "return_c")
    x0 = (w0.astype(F32) + e0).astype(BF16)
    f0, f1 = chunks([(1, 0), (-1, 1)], v1, "return_d")
    x1 = (w1.astype(F32) + after(e1, x0)).astype(BF16)
    u0, u1, w0, w1 = shift(v0, 0), shift(v1, 1), shift(x0, 0), shift(x1, 1)
    v0 = (u0.astype(F32) + f0).astype(BF16)
    v1 = (u1.astype(F32) + f1).astype(BF16)
    up = (shift(v0, 0), shift(v1, 1))
    down = (w0, w1)

    def mix_out(keep0, keep1, got0, got1, scale, out):
        q = lax.axis_index("col")
        for k, (keep, got) in enumerate(((keep0, got0), (keep1, got1))):
            mixed = over(scale[node_piece(k), :]) * (keep[...] + got[...].astype(F32))
            mixed = mixed.reshape(blocks // 2, 2, half, width)
            mixed = jnp.where(q == 0, mixed[:, 0], mixed[:, 1]).reshape(hshape)
            out[k * hrows : (k + 1) * hrows, :] = (mixed * jax.nn.sigmoid(mixed)).astype(BF16)

    output = call(
        mix_out, array(shape, BF16), [VM] * 5, (*keep, *got, after(scale_all, v1)), "mix_out"
    )

    def finish(base0, base1, g0, r1, g1, r0, sc, w, out_hbm, out, sems):
        copies = []
        step = hrows // 2
        for h, (base, g, r) in enumerate(((base0, g0, r0), (base1, g1, r1))):
            for i in range(2):
                at = slice(i * step, (i + 1) * step)
                whole = slice(h * hrows + i * step, h * hrows + (i + 1) * step)
                total = base[at, :] + g[at, :].astype(F32) + r[at, :].astype(F32)
                comb = (over(sc[whole, :]) * total).astype(BF16)
                out[whole, :] = lax.dot_general(
                    comb, w[...], (((1,), (1,)), ((), ())), preferred_element_type=F32
                ).astype(BF16)
                to = pl.ds(h * hrows + i * step, step)
                copies.append(pltpu.make_async_copy(out.at[to], out_hbm.at[to], sems.at[2 * h + i]))
                copies[-1].start()
        for c in copies:
            c.wait()

    grad = pl.pallas_call(
        finish,
        out_shape=array(shape, BF16),
        in_specs=[VM] * 8,
        out_specs=ANY,
        scratch_shapes=[pltpu.VMEM(shape, BF16), pltpu.SemaphoreType.DMA((4,))],
        cost_estimate=pl.CostEstimate(flops=0, bytes_accessed=0, transcendentals=0),
        compiler_params=pltpu.CompilerParams(vmem_limit_bytes=24 * 2**20),
        name="finish",
    )(*base, *up, *down, scale, weight)
    return output.reshape(feats.shape), grad.reshape(feats.shape)


def shards(feats, weight, degree, tile_cols, adjacency, cotangent):
    n = lax.axis_size("row")
    blocks, half, width = feats.shape
    dense = (
        n * blocks <= blocks * tile_cols.shape[1]
        and n % 2 == 0
        and n == 8
        and blocks % 2 == 0
        and blocks <= 16
        and half % 16 == 0
        and width % 128 == 0
        and adjacency.shape[2] == 2 * half
        and lax.axis_size("col") == 2
    )
    plan = dense_plan if dense else sparse_plan
    return plan(feats, weight, degree, tile_cols, adjacency, cotangent)


def solution(mesh):
    in_specs = (
        P(("grp", "row"), "col", None),
        P(),
        P(("grp", "row"), "col"),
        P(("grp", "row"), None),
        P(("grp", "row"), "col", None),
        P(("grp", "row"), "col", None),
    )
    out_specs = (P(("grp", "row"), "col", None), P(("grp", "row"), "col", None))
    return jax.shard_map(shards, mesh=mesh, in_specs=in_specs, out_specs=out_specs, check_vma=False)
```

```python
import functools

import jax
import jax.numpy as jnp
from jax import lax
from jax.experimental import pallas as pl
from jax.experimental.pallas import tpu as pltpu
from jax.sharding import PartitionSpec as P

F32 = jnp.float32
BF16 = jnp.bfloat16


def sparse_plan(feats, weight, degree, tile_cols, adjacency, cotangent):
    blocks, half_rows, feat_width = feats.shape
    slots_per = tile_cols.shape[1]
    tile_side = adjacency.shape[2]
    peer_count = lax.axis_size("row")
    tile_count = blocks * slots_per
    per_peer = (tile_count + peer_count - 1) // peer_count
    capacity = peer_count * per_peer
    columns = tile_cols.reshape(tile_count)
    is_live = columns >= 0
    owners = jnp.where(is_live, columns // blocks, -1)
    local_block = jnp.where(is_live, columns % blocks, -1)
    earlier = jnp.arange(tile_count)[:, None] > jnp.arange(tile_count)[None, :]
    same_owner = (owners[:, None] == owners[None, :]) & earlier & is_live[None, :]
    tile_rank = jnp.sum(same_owner.astype(jnp.int32), axis=1)
    target_slot = jnp.where(is_live, owners * per_peer + tile_rank, capacity)
    wanted = jnp.zeros((capacity,), jnp.int32).at[target_slot].set(local_block + 1, mode="drop")
    wanted = wanted.reshape(peer_count, per_peer)
    received = lax.all_to_all(wanted, "row", split_axis=0, concat_axis=0, tiled=True)
    incoming = received - 1
    scaling = lax.rsqrt(degree.astype(F32) + 1.0)[..., None]
    projected = jnp.dot(
        feats.reshape(blocks * half_rows, feat_width), weight, preferred_element_type=F32
    )
    sent_rows = (scaling * projected.reshape(blocks, half_rows, feat_width)).astype(BF16)
    tiles_bf = adjacency.astype(BF16).reshape(blocks, slots_per, half_rows, tile_side)
    pick_index = jnp.where(incoming < 0, blocks, incoming)
    replies = jnp.take(sent_rows, pick_index, axis=0, mode="fill", fill_value=0)
    fetched = lax.all_to_all(replies, "row", split_axis=0, concat_axis=0, tiled=True).reshape(
        capacity, half_rows, feat_width
    )
    tile_feats = jnp.take(fetched, target_slot, axis=0, mode="fill", fill_value=0)
    tile_feats = tile_feats.reshape(blocks, slots_per, half_rows, feat_width)
    gathered = lax.dot_general(
        tiles_bf, tile_feats, (((1, 2), (1, 2)), ((0,), (0,))), preferred_element_type=F32
    )
    own_rows = lax.psum_scatter(gathered, "col", scatter_dimension=1, tiled=True)
    mixed = scaling * (own_rows + sent_rows.astype(F32))
    sigmoid_z = jax.nn.sigmoid(mixed)
    output = (mixed * sigmoid_z).astype(BF16)
    silu_slope = sigmoid_z * (1.0 + mixed * (1.0 - sigmoid_z))
    back_sent = (scaling * cotangent.astype(F32) * silu_slope).astype(BF16)
    full_rows = lax.all_gather(back_sent, "col", axis=1, tiled=True)
    partials = lax.dot_general(
        tiles_bf, full_rows, (((3,), (1,)), ((0,), (0,))), preferred_element_type=F32
    )
    outgoing = jnp.zeros((capacity, half_rows, feat_width), F32)
    outgoing = outgoing.at[target_slot].set(
        partials.reshape(tile_count, half_rows, feat_width), mode="drop"
    )
    outgoing = outgoing.reshape(peer_count, per_peer, half_rows, feat_width)
    arrived = lax.all_to_all(outgoing, "row", split_axis=0, concat_axis=0, tiled=True).reshape(
        capacity, half_rows, feat_width
    )
    selector = (incoming.reshape(capacity)[:, None] == jnp.arange(blocks)[None, :]).astype(F32)
    returned = jnp.einsum("sl,sjf->ljf", selector, arrived, precision=lax.Precision.HIGHEST)
    combined = (scaling * (returned + back_sent.astype(F32))).astype(BF16)
    grad_rows = jnp.dot(
        combined.reshape(blocks * half_rows, feat_width), weight.T, preferred_element_type=F32
    )
    return (output, grad_rows.astype(BF16).reshape(blocks, half_rows, feat_width))


VM = pl.BlockSpec(memory_space=pltpu.VMEM)
ANY = pl.BlockSpec(memory_space=pl.ANY)
OTHER = [(0, 1), (1, 0)]


def call(body, outs, ins, args, name, **kw):
    return pl.pallas_call(
        body,
        out_shape=outs,
        in_specs=ins,
        out_specs=jax.tree.map(lambda _: VM, outs),
        cost_estimate=pl.CostEstimate(flops=0, bytes_accessed=0, transcendentals=0),
        compiler_params=pltpu.CompilerParams(vmem_limit_bytes=24 * 2**20),
        name=name,
        **kw,
    )(*args)


def array(shape, dtype):
    return jax.ShapeDtypeStruct(shape, dtype)


def after(value, *tokens):
    return lax.optimization_barrier((value,) + tokens)[0]


def dense_plan(feats, weight, degree, tile_cols, adjacency, cotangent):
    blocks, half, width = feats.shape
    slots = tile_cols.shape[1]
    side = adjacency.shape[2]
    n = lax.axis_size("row")
    rows = blocks * half
    hrows = rows // 2
    span = blocks * side
    far = n // 2
    ring = [2 * p if p < far else 2 * (n - 1 - p) + 1 for p in range(n)]
    fwd = [(ring[p], ring[(p + 1) % n]) for p in range(n)]
    bwd = [(b, a) for a, b in fwd]

    def half_rows_of(d, h):
        me = lax.axis_index("row")
        z = lax.shift_right_logical(me, 1)
        place = jnp.where(lax.rem(me, 2) == 0, z, n - 1 - z)
        p = lax.rem(place + (d + n), n)
        owner = jnp.where(p < far, 2 * p, 2 * (n - 1 - p) + 1)
        return pl.ds(pl.multiple_of(owner * rows + h * hrows, hrows), hrows)

    def scale_columns(degree_values):
        scale = lax.rsqrt(degree_values.astype(F32) + 1.0)
        eye = lax.broadcasted_iota(jnp.int32, (half, half), 0) == lax.broadcasted_iota(
            jnp.int32, (half, half), 1
        )
        for b in range(blocks):
            line = jnp.broadcast_to(scale[b : b + 1, :], (half, half))
            column = jnp.sum(jnp.where(eye, line, 0.0), axis=1, keepdims=True)
            yield b, jnp.broadcast_to(column, (half, 128))

    def over(scale):
        return jnp.tile(scale, (1, width // 128))

    def project(deg_hbm, x_hbm, w_hbm, s0, s1, sc, deg, x, w, sems):
        deg_copy = pltpu.make_async_copy(deg_hbm, deg, sems.at[0])
        deg_copy.start()
        copies = []
        for src, dst, parts in ((x_hbm, x, 4), (w_hbm, w, 2)):
            step = src.shape[0] // parts
            for i in range(parts):
                at = pl.ds(i * step, step)
                copies.append(
                    pltpu.make_async_copy(src.at[at], dst.at[at], sems.at[1 + len(copies)])
                )
                copies[-1].start()
        deg_copy.wait()
        for b, column in scale_columns(deg[...]):
            sc[b * half : (b + 1) * half, :] = column
        for c in copies:
            c.wait()
        proj = jnp.dot(x[...], w[...], preferred_element_type=F32)
        out = (over(sc[...]) * proj).astype(BF16)
        s0[...] = out[:hrows]
        s1[...] = out[hrows:]

    hshape = (hrows, width)
    s0, s1, scale = call(
        project,
        (array(hshape, BF16), array(hshape, BF16), array((rows, 128), F32)),
        [ANY] * 3,
        tuple(
            pltpu.with_memory_space_constraint(a, pltpu.HBM)
            for a in (degree, feats.reshape(rows, width), weight)
        ),
        "project",
        scratch_shapes=[
            pltpu.VMEM(degree.shape, jnp.int32),
            pltpu.VMEM((rows, width), BF16),
            pltpu.VMEM(weight.shape, BF16),
            pltpu.SemaphoreType.DMA((7,)),
        ],
    )

    def densify(cols_hbm, adj_hbm, deg_hbm, cot_hbm, dense, pack, cols, adj, deg, sems):
        def tiles_of(b):
            return pl.ds(b * slots, slots)

        cols_copy = pltpu.make_async_copy(cols_hbm, cols, sems.at[blocks])
        deg_copy = pltpu.make_async_copy(deg_hbm, deg, sems.at[blocks + 1])
        cot_copy = pltpu.make_async_copy(cot_hbm, pack.at[pl.ds(0, rows)], sems.at[blocks + 2])
        cols_copy.start()
        deg_copy.start()
        copies = [
            pltpu.make_async_copy(adj_hbm.at[tiles_of(b)], adj.at[tiles_of(b)], sems.at[b])
            for b in range(blocks)
        ]
        for c in copies:
            c.start()
        cot_copy.start()
        dense[...] = jnp.zeros(dense.shape, BF16)
        pack[rows:, :] = jnp.zeros((16, width), BF16)
        deg_copy.wait()
        padded = jnp.concatenate([deg[...], jnp.zeros((16 - blocks, half), jnp.int32)], axis=0)
        pack[rows:, :half] = padded.astype(F32).astype(BF16)
        cols_copy.wait()
        for b in range(blocks):
            copies[b].wait()
            lanes = slice(b * side, (b + 1) * side)
            for k in range(slots):
                c = cols[b, k]
                tile = jnp.where(c >= 0, adj[b * slots + k], 0).astype(F32).astype(BF16)
                place = pl.ds(pl.multiple_of(jnp.maximum(c, 0) * half, half), half)
                dense[place, lanes] = dense[place, lanes] + tile
        cot_copy.wait()

    def hbm(x):
        return pltpu.with_memory_space_constraint(x, pltpu.HBM)

    shape = (rows, width)
    dense, pack = pl.pallas_call(
        densify,
        out_shape=(pltpu.VMEM((n * rows, span), BF16), array((rows + 16, width), BF16)),
        in_specs=[ANY] * 4,
        out_specs=(VM, VM),
        scratch_shapes=[
            pltpu.SMEM(tile_cols.shape, jnp.int32),
            pltpu.VMEM(adjacency.shape, jnp.int32),
            pltpu.VMEM(degree.shape, jnp.int32),
            pltpu.SemaphoreType.DMA((blocks + 3,)),
        ],
        cost_estimate=pl.CostEstimate(flops=0, bytes_accessed=0, transcendentals=0),
        compiler_params=pltpu.CompilerParams(vmem_limit_bytes=24 * 2**20),
        name="densify",
    )(hbm(tile_cols), hbm(adjacency), hbm(degree), hbm(cotangent.reshape(shape)))

    def shift_pair(pair):
        return lax.ppermute(pair[0], "row", fwd), lax.ppermute(pair[1], "row", bwd)

    def gather_terms(dense, items):
        total = None
        for d, h, ref in items:
            term = lax.dot_general(
                ref[...], dense[half_rows_of(d, h), :], (((0,), (0,)), ((), ())),
                preferred_element_type=F32,
            )
            total = term if total is None else total + term
        return total

    def gather(items, part, name):
        def body(dense, *refs):
            total = gather_terms(dense, [(d, h, r) for (d, h, _), r in zip(items, refs)])
            refs[-1][...] = total if part is None else refs[-2][...] + total

        extra = () if part is None else (part,)
        return call(
            body,
            array((width, span), F32),
            [VM] * (1 + len(items) + len(extra)),
            (dense, *[i[2] for i in items], *extra),
            name,
        )

    long, short = [(s0, s1)], [(s1, s0)]
    long.append(shift_pair(long[0]))
    short.append(shift_pair(short[0]))

    long[1] = (after(long[1][0], dense), after(long[1][1], dense))
    long.append(shift_pair(long[1]))
    short.append(shift_pair(short[1]))
    long.append(shift_pair(long[2]))
    def long_items(hop):
        return [(-hop, 0, long[hop][0]), (hop, 1, long[hop][1])]

    def short_items(hop):
        return [(-hop, 1, short[hop][0]), (hop, 0, short[hop][1])]

    peer_pack = lax.ppermute(pack, "col", OTHER)

    def prepare(pack, peer_pack, scale, scaled):
        mine = lax.axis_index("col")
        for h, p in ((mine, pack), (1 - mine, peer_pack)):
            degrees = p[rows:, :half].astype(F32)[:blocks]
            for b, column in scale_columns(degrees):
                scale[b, h] = column
                scaled[b, h] = over(column) * p[b * half : (b + 1) * half, :].astype(F32)

    scale_all, scaled_cot = call(
        prepare,
        (array((blocks, 2, half, 128), F32), array((blocks, 2, half, width), F32)),
        [VM] * 2,
        (pack, peer_pack),
        "prepare",
    )
    scale_all = scale_all.reshape(span, 128)
    scaled_cot = scaled_cot.reshape(span, width)

    part = gather([(0, 0, s0), (0, 1, s1)] + long_items(1), None, "gather_near")
    short.append(shift_pair(short[2]))
    long[3] = (after(long[3][0], part), long[3][1])
    part = gather(short_items(1) + long_items(2), part, "gather_two")
    long[3] = (long[3][0], after(long[3][1], part))
    long.append(shift_pair(long[3]))
    part = gather(short_items(2) + long_items(3), after(part, scale_all), "gather_three")

    def turn(dense, fa, ba, part, s0, s1, whole, wide):
        total = part[...] + gather_terms(dense, [(-(far - 1), 1, fa), (far - 1, 0, ba)])
        whole[...] = total.T.reshape(blocks, 2, half, width)
        q = lax.axis_index("col")
        for b in range(blocks):
            at = (b * half) % hrows
            own = s0 if b < blocks // 2 else s1
            whole[b, q] = whole[b, q] + own[at : at + half, :].astype(F32)
        for h in range(2):
            wide[:, h * hrows : (h + 1) * hrows] = dense[half_rows_of(far, h), :].T

    part, turned = call(
        turn,
        (array((blocks, 2, half, width), F32), array((span, rows), BF16)),
        [VM] * 6,
        (dense, *short[3], part, s0, s1),
        "turn",
    )
    part = part.reshape(span, width)

    def node_piece(k):
        return slice(k * rows, (k + 1) * rows)

    everyone = (span, width)

    def last(part, turned, fa, ba, keep, give):
        total = part[...] + jnp.dot(turned[:, :hrows], fa[...], preferred_element_type=F32)
        total = total + jnp.dot(turned[:, hrows:], ba[...], preferred_element_type=F32)
        give[...] = total.astype(BF16)
        keep[...] = total

    keep, give = call(
        last,
        (array(everyone, F32), array(everyone, BF16)),
        [VM] * 4,
        (part, turned, *long[far]),
        "gather_last",
    )
    got = lax.ppermute(give, "col", OTHER)

    def back_of(k, keep, got, scale, scaled):
        at = node_piece(k)
        mixed = over(scale[at, :]) * (keep[at, :] + got[at, :].astype(F32))
        sig = jax.nn.sigmoid(mixed)
        slope = sig * (1.0 + mixed * (1.0 - sig))
        return (scaled[at, :] * slope).astype(BF16)

    def far_term(k, dense, back):
        at = pl.ds(half_rows_of(far, 0).start, rows)
        return jnp.dot(dense[at, node_piece(k)], back, preferred_element_type=F32)

    def mix(keep, got, scale, scaled, dense, back0, back1, c0, c1):
        out = None
        for k, back in enumerate((back0, back1)):
            value = back_of(k, keep, got, scale, scaled)
            back[...] = value
            term = far_term(k, dense, value)
            out = term if out is None else out + term
        c0[...] = out[:hrows].astype(BF16)
        c1[...] = out[hrows:].astype(BF16)

    back0, back1, *up = call(
        mix,
        (array(shape, BF16),) * 2 + (array(hshape, BF16),) * 2,
        [VM] * 5,
        (keep, got, scale_all, scaled_cot, dense),
        "mix",
    )
    back = [back0, back1]
    token = up[0]
    up = shift_pair(up)

    def chunk(dense, back, d, h):
        at = half_rows_of(d, h)
        return sum(
            jnp.dot(dense[at, node_piece(k)], back[k][...], preferred_element_type=F32)
            for k in range(2)
        )

    def chunks(which, token, name, dtype=F32):
        def body(dense, *refs):
            for (d, h), out in zip(which, refs[2:]):
                out[...] = chunk(dense, refs[:2], d, h).astype(dtype)

        return call(
            body,
            tuple(array(hshape, dtype) for _ in which),
            [VM] * 3,
            (dense, after(back[0], token), back[1]),
            name,
        )

    def add(total, term, token):
        return (total.astype(F32) + term).astype(BF16)

    def shift(x, h):
        return lax.ppermute(x, "row", (fwd, bwd)[h])

    down = chunks([(far - 1, 1), (1 - far, 0)], token, "return_next", BF16)
    token = down[0]
    down = shift_pair(down)
    a0, a1, c0, c1, d0, d1 = chunks([(3, 0), (-3, 1), (2, 1), (-2, 0), (2, 0), (-2, 1)], token, "return_ab")
    u0 = (up[0].astype(F32) + a0).astype(BF16)
    u1 = (up[1].astype(F32) + a1).astype(BF16)
    w0 = (down[0].astype(F32) + after(c0, u0, u1)).astype(BF16)
    def own_base(dense, back0, back1, base0, base1):
        q = lax.axis_index("col")
        for h, (back, base) in enumerate(((back0, base0), (back1, base1))):
            mine = back[...].reshape(blocks // 2, 2, half, width)
            mine = jnp.where(q == 0, mine[:, 0], mine[:, 1]).reshape(hshape).astype(F32)
            base[...] = chunk(dense, (back0, back1), 0, h) + mine

    base = call(
        own_base,
        (array(hshape, F32), array(hshape, F32)),
        [VM] * 3,
        (dense, after(back[0], w0), back[1]),
        "own_base",
    )
    w1 = (down[1].astype(F32) + c1).astype(BF16)
    u0, u1, w0, w1 = shift(u0, 0), shift(u1, 1), shift(w0, 0), shift(w1, 1)
    v0 = (u0.astype(F32) + d0).astype(BF16)
    v1 = (u1.astype(F32) + d1).astype(BF16)
    e0, e1 = chunks([(1, 1), (-1, 0)], v0, "return_c")
    x0 = (w0.astype(F32) + e0).astype(BF16)
    f0, f1 = chunks([(1, 0), (-1, 1)], v1, "return_d")
    x1 = (w1.astype(F32) + after(e1, x0)).astype(BF16)
    u0, u1, w0, w1 = shift(v0, 0), shift(v1, 1), shift(x0, 0), shift(x1, 1)
    v0 = (u0.astype(F32) + f0).astype(BF16)
    v1 = (u1.astype(F32) + f1).astype(BF16)
    up = (shift(v0, 0), shift(v1, 1))
    down = (w0, w1)

    def mix_out(keep, got, scale, out):
        q = lax.axis_index("col")
        for k in range(2):
            at = node_piece(k)
            mixed = over(scale[at, :]) * (keep[at, :] + got[at, :].astype(F32))
            mixed = mixed.reshape(blocks // 2, 2, half, width)
            mixed = jnp.where(q == 0, mixed[:, 0], mixed[:, 1]).reshape(hshape)
            out[k * hrows : (k + 1) * hrows, :] = (mixed * jax.nn.sigmoid(mixed)).astype(BF16)

    output = call(
        mix_out, array(shape, BF16), [VM] * 3, (keep, got, after(scale_all, v1)), "mix_out"
    )

    def finish(base0, base1, g0, r1, g1, r0, sc, w, out_hbm, out, sems):
        copies = []
        step = hrows // 2
        for h, (base, g, r) in enumerate(((base0, g0, r0), (base1, g1, r1))):
            for i in range(2):
                at = slice(i * step, (i + 1) * step)
                whole = slice(h * hrows + i * step, h * hrows + (i + 1) * step)
                total = base[at, :] + g[at, :].astype(F32) + r[at, :].astype(F32)
                comb = (over(sc[whole, :]) * total).astype(BF16)
                out[whole, :] = lax.dot_general(
                    comb, w[...], (((1,), (1,)), ((), ())), preferred_element_type=F32
                ).astype(BF16)
                to = pl.ds(h * hrows + i * step, step)
                copies.append(pltpu.make_async_copy(out.at[to], out_hbm.at[to], sems.at[2 * h + i]))
                copies[-1].start()
        for c in copies:
            c.wait()

    grad = pl.pallas_call(
        finish,
        out_shape=array(shape, BF16),
        in_specs=[VM] * 8,
        out_specs=ANY,
        scratch_shapes=[pltpu.VMEM(shape, BF16), pltpu.SemaphoreType.DMA((4,))],
        cost_estimate=pl.CostEstimate(flops=0, bytes_accessed=0, transcendentals=0),
        compiler_params=pltpu.CompilerParams(vmem_limit_bytes=24 * 2**20),
        name="finish",
    )(*base, *up, *down, scale, weight)
    return output.reshape(feats.shape), grad.reshape(feats.shape)


def shards(feats, weight, degree, tile_cols, adjacency, cotangent):
    n = lax.axis_size("row")
    blocks, half, width = feats.shape
    dense = (
        n * blocks <= blocks * tile_cols.shape[1]
        and n % 2 == 0
        and n == 8
        and blocks % 2 == 0
        and blocks <= 16
        and half % 16 == 0
        and width % 128 == 0
        and adjacency.shape[2] == 2 * half
        and lax.axis_size("col") == 2
    )
    plan = dense_plan if dense else sparse_plan
    return plan(feats, weight, degree, tile_cols, adjacency, cotangent)


def solution(mesh):
    in_specs = (
        P(("grp", "row"), "col", None),
        P(),
        P(("grp", "row"), "col"),
        P(("grp", "row"), None),
        P(("grp", "row"), "col", None),
        P(("grp", "row"), "col", None),
    )
    out_specs = (P(("grp", "row"), "col", None), P(("grp", "row"), "col", None))
    return jax.shard_map(shards, mesh=mesh, in_specs=in_specs, out_specs=out_specs, check_vma=False)
```
